32 devices in a mesh: dp: 4 (over y, x), ctx: 8 (over z, core).
Axes of the slice: x: 2, y: 2, z: 4, core: 2. Of those that a mesh axis runs over, the one named last changes fastest.
Arguments:
- queries: bfloat16 [8192, 4096], P(('dp', 'ctx')), may hold values from -5 to 5
- conv_keys: bfloat16 [8192, 512], P(('dp', 'ctx')), may hold values from -5 to 5
- conv_values: bfloat16 [8192, 512], P(('dp', 'ctx')), may hold values from -5 to 5
- out_grad: bfloat16 [8192, 4096], P(('dp', 'ctx')), may hold values from -5 to 5
- segment_ids: int32 [32, 256], P(('dp', 'ctx')), may hold values from 0 to 2, never falling along the last dimension, each value on 1 to 128 neighbouring positions
- cart_keys: bfloat16 [256, 512], P('ctx'), may hold values from -5 to 5
- cart_values: bfloat16 [256, 512], P('ctx'), may hold values from -5 to 5
Outputs:
- cart_key_grad: float32 [256, 512], P('ctx')
- cart_value_grad: float32 [256, 512], P('ctx')
The draws below stay inside these ranges and needn't reach their ends.
Inputs may be any that keep to these rules, and one draw needn't show every extreme that they name: `segment_ids`: within a block the numbers never fall; each block holds 3 conversations of 1 to 128 tokens, one of exactly 128.
All inputs are finite; a program needn't handle non-finite values.
Results may differ from the reference program's by a relative error of at most 0.0041.
Values may be sent and summed in bfloat16 or wider, within the bound.
A program may use at most 128 MiB of HBM per device.

```python
import math
import jax
import jax.numpy as jnp
import numpy as np
from jax import lax

HQ = 32
HK = 4
HD = 128
TOK_DEV = 256
BLOCKS = 32
TOKENS = 8192
CART = 256


def draw_cart_keys(key, part):
    key = jax.random.fold_in(key, 11)
    result = jnp.clip(jax.random.normal(key, (CART, HK * HD), jnp.float32), -5.0, 5.0)
    return result.astype(jnp.bfloat16)


def draw_queries(key, part):
    key = jax.random.fold_in(key, 23)
    result = jnp.clip(jax.random.normal(key, (TOKENS, HQ * HD), jnp.float32), -5.0, 5.0)
    return result.astype(jnp.bfloat16)


def shard_levels(rng, dims, shards, least, largest):
    level = 1.0
    for dim, shards_of in shards:
        draws = jax.random.uniform(jax.random.fold_in(jax.random.fold_in(rng, 6), dim), (shards_of,), jnp.float32, least / len(shards), largest / len(shards))
        level = level * jnp.repeat(jnp.exp(draws), dims[dim] // shards_of).reshape((-1,) + (1,) * (len(dims) - 1 - dim))
    return level


def split_up(number_of, total, bound, lean):
    portions = [(1 << 20) // math.isqrt(standing ** lean) + 1 for standing in range(2, number_of + 1)]
    surplus, counts = total - bound - (number_of - 1), [1] * (number_of - 1)
    while surplus > 0:
        candidates = [i for i in range(number_of - 1) if counts[i] < bound]
        pool, remaining = sum([portions[i] for i in candidates]), surplus
        for i in candidates:
            more = min(bound - counts[i], max(1, remaining * portions[i] // pool), surplus)
            counts[i] = counts[i] + more
            surplus = surplus - more
    return np.array([bound] + counts)


def ragged(stream_key, amount, total, limit, lean):
    if amount == 2:
        one = jax.random.randint(stream_key, (), max(1, total - limit), min(limit, total - 1) + 1)
        return jnp.stack([one, total - one])
    sizes = jnp.asarray(split_up(amount, total, limit, lean), jnp.int32)
    pairs = (amount - 1) // 2
    donor, receiver = sizes[1:1 + 2 * pairs:2], sizes[2:2 + 2 * pairs:2]
    room = jnp.minimum(donor - 1, limit - receiver)
    passed = jax.random.randint(jax.random.fold_in(stream_key, 1), (pairs,), 0, 1 << 20) % (room + 1)
    sizes = sizes.at[1:1 + 2 * pairs:2].set(donor - passed).at[2:2 + 2 * pairs:2].set(receiver + passed)
    return sizes[jax.random.permutation(jax.random.fold_in(stream_key, 2), amount)]


def noise(own_key, shape, width, bound, split=(), dtype=jnp.bfloat16):
    entries = width * jax.random.normal(own_key, shape, jnp.float32)
    if split:
        entries = entries * shard_levels(own_key, shape, split, -0.22, 0.18)
    return jnp.clip(entries, -bound, bound).astype(dtype)


def setup_inputs(seed: int = 0) -> dict:
    seeds = jax.random.split(jax.random.key(seed), 8)
    queries = draw_queries(jax.random.fold_in(seeds[7], 71), 0)
    conv_keys = noise(seeds[1], (TOKENS, HK * HD), 1.0, 5.0, ((0, 32),))
    conv_values = noise(seeds[2], (TOKENS, HK * HD), 1.0, 5.0, ((0, 32),))
    out_grad = noise(seeds[3], (TOKENS, HQ * HD), 1.0, 5.0, ((0, 32),))
    segment_ids = jax.vmap(lambda own: jnp.searchsorted(jnp.cumsum(ragged(own, 3, TOK_DEV, TOK_DEV // 2, 0)), jnp.arange(TOK_DEV), side="right"))(jax.random.split(seeds[4], BLOCKS)).reshape((BLOCKS, TOK_DEV)).astype(jnp.int32)
    cart_keys = draw_cart_keys(jax.random.fold_in(seeds[7], 71), 0)
    cart_values = noise(seeds[6], (CART, HK * HD), 1.0, 5.0, ((0, 8),))
    return {"queries": queries, "conv_keys": conv_keys, "conv_values": conv_values, "out_grad": out_grad, "segment_ids": segment_ids, "cart_keys": cart_keys, "cart_values": cart_values}


def block_terms(queries, conv_keys, conv_values, out_grad, segments, cart_keys, cart_values):
    scale = 1.0 / math.sqrt(HD)
    group = HQ // HK
    position = jnp.arange(TOK_DEV)
    allowed = (segments[:, None] == segments[None, :]) & (position[None, :] <= position[:, None])
    key_parts = []
    value_parts = []
    for head_group in range(HK):
        low = head_group * group * HD
        high = (head_group + 1) * group * HD
        query_group = queries[:, low:high].reshape(TOK_DEV, group, HD).astype(jnp.float32)
        grad_group = out_grad[:, low:high].reshape(TOK_DEV, group, HD).astype(jnp.float32)
        cols = slice(head_group * HD, (head_group + 1) * HD)
        cart_key = cart_keys[:, cols].astype(jnp.float32)
        cart_value = cart_values[:, cols].astype(jnp.float32)
        conv_key = conv_keys[:, cols].astype(jnp.float32)
        conv_value = conv_values[:, cols].astype(jnp.float32)
        score_cart = jnp.einsum('tgd,jd->tgj', query_group, cart_key) * scale
        score_conv = jnp.einsum('tgd,ud->tgu', query_group, conv_key) * scale
        score_conv = jnp.where(allowed[:, None, :], score_conv, -jnp.inf)
        top = jnp.maximum(lax.optimization_barrier(jnp.max(score_cart, axis=-1)), lax.optimization_barrier(jnp.max(score_conv, axis=-1)))
        exp_cart = jnp.exp(score_cart - top[..., None])
        exp_conv = jnp.exp(score_conv - top[..., None])
        total = lax.optimization_barrier(jnp.sum(exp_cart, axis=-1)) + lax.optimization_barrier(jnp.sum(exp_conv, axis=-1))
        probs_cart = exp_cart / total[..., None]
        probs_conv = exp_conv / total[..., None]
        rounded_cart = probs_cart.astype(jnp.bfloat16).astype(jnp.float32)
        rounded_conv = probs_conv.astype(jnp.bfloat16).astype(jnp.float32)
        mixed = jnp.einsum('tgj,jd->tgd', rounded_cart, cart_value) + jnp.einsum('tgu,ud->tgd', rounded_conv, conv_value)
        delta = lax.optimization_barrier(jnp.sum(grad_group * mixed, axis=-1))
        dprob = jnp.einsum('tgd,jd->tgj', grad_group, cart_value)
        dscore = probs_cart * (dprob - delta[..., None])
        dscore_b = dscore.astype(jnp.bfloat16).astype(jnp.float32)
        value_parts.append(jnp.einsum('tgj,tgd->jd', rounded_cart, grad_group))
        key_parts.append(jnp.einsum('tgj,tgd->jd', dscore_b, query_group) * scale)
    return jnp.concatenate(key_parts + value_parts, axis=1)

def reference(queries, conv_keys, conv_values, out_grad, segment_ids, cart_keys, cart_values):
    items = (queries.reshape(BLOCKS, TOK_DEV, HQ * HD), conv_keys.reshape(BLOCKS, TOK_DEV, HK * HD), conv_values.reshape(BLOCKS, TOK_DEV, HK * HD), out_grad.reshape(BLOCKS, TOK_DEV, HQ * HD), segment_ids)

    def step(carry, block):
        return (carry + block_terms(block[0], block[1], block[2], block[3], block[4], cart_keys, cart_values), None)
    start = jnp.zeros((CART, 2 * HK * HD), jnp.float32)
    summed = lax.scan(step, start, items)[0]
    return (summed[:, :HK * HD], summed[:, HK * HD:])
```

```python
import functools
import math

import jax
import jax.numpy as jnp
from jax import lax
from jax.experimental import pallas as pl
from jax.experimental.pallas import tpu as pltpu
from jax.sharding import PartitionSpec as P

HD = 128
MESH = pl.DeviceIdType.MESH
NT = (((1,), (1,)), ((), ()))


def dot_nt(a, b):
    return lax.dot_general(a, b, NT, preferred_element_type=jnp.float32)


def dot(a, b):
    return jnp.dot(a, b, preferred_element_type=jnp.float32)


def kernel(
    n, nd, groups, heads,
    q_hbm, ck_hbm, cv_hbm, og_hbm, seg_hbm, kk_hbm, kv_hbm,
    dk_ref, dv_ref,
    q_s, og_s, ck_s, cv_s, seg_s, bias, stats, buf, part, r1, s2, r2, r3,
    in_sem, conv_sem, cart_sem,
    g_send, g_recv, f_send, f_recv, s1_send, s1_recv, s2_send, s2_recv, s3_send, s3_recv,
):
    dp, me = lax.axis_index("dp"), lax.axis_index("ctx")
    half = n // 2
    core = lax.rem(me, 2)
    place = me // 2
    sibling = me + 1 - 2 * core
    tokens = q_s.shape[0]
    rows = buf.shape[2]
    cart = n * rows
    width = heads * HD
    scale = 1.0 / math.sqrt(HD)
    factor = scale * math.log2(math.e)

    barrier = pltpu.get_barrier_semaphore()
    pl.semaphore_signal(barrier, inc=1, device_id=(dp, sibling), device_id_type=MESH)
    for i in range(1, half):
        pl.semaphore_signal(
            barrier, inc=1, device_id=(dp, lax.rem(me + 2 * i, n)), device_id_type=MESH
        )
    for i in range(1, nd):
        pl.semaphore_signal(
            barrier, inc=1, device_id=(lax.rem(dp + i, nd), me), device_id_type=MESH
        )

    cart_copies = []
    for g in range(groups):
        cols = pl.ds(g * HD, HD)
        cart_copies.append(
            pltpu.make_async_copy(kk_hbm.at[:, cols], buf.at[me, g], cart_sem.at[g])
        )
        cart_copies.append(
            pltpu.make_async_copy(
                kv_hbm.at[:, cols], buf.at[me, groups + g], cart_sem.at[groups + g]
            )
        )
    for copy in cart_copies:
        copy.start()
    conv_copies = [
        pltpu.make_async_copy(seg_hbm, seg_s, conv_sem.at[0]),
        pltpu.make_async_copy(ck_hbm, ck_s, conv_sem.at[1]),
        pltpu.make_async_copy(cv_hbm, cv_s, conv_sem.at[2]),
    ]
    for copy in conv_copies:
        copy.start()
    in_copies = []
    for g in range(groups):
        cols = pl.ds(g * width, width)
        in_copies.append(
            (
                pltpu.make_async_copy(q_hbm.at[:, cols], q_s.at[:, cols], in_sem.at[0, g]),
                pltpu.make_async_copy(og_hbm.at[:, cols], og_s.at[:, cols], in_sem.at[1, g]),
            )
        )
        for copy in in_copies[-1]:
            copy.start()
    for copy in cart_copies:
        copy.wait()
    pl.semaphore_wait(barrier, 1 + (half - 1) + (nd - 1))

    def remote(src, dst, send, recv, target):
        return pltpu.make_async_remote_copy(
            src_ref=src, dst_ref=dst, send_sem=send, recv_sem=recv,
            device_id=target, device_id_type=MESH,
        )

    gather = [
        remote(
            buf.at[me], buf.at[me], g_send.at[i], g_recv.at[i], (dp, lax.rem(me + 2 * i, n))
        )
        for i in range(1, half)
    ]
    arrivals = [lax.rem(me + n - 2 * i, n) for i in range(half)]
    forward = [
        remote(buf.at[a], buf.at[a], f_send.at[i], f_recv.at[i], (dp, sibling))
        for i, a in enumerate(arrivals)
    ]
    for copy in gather:
        copy.start()
    forward[0].start()

    for copy in conv_copies:
        copy.wait()
    seg_row = jnp.broadcast_to(seg_s[...].astype(jnp.float32), (tokens, tokens))
    key_at = lax.broadcasted_iota(jnp.int32, (tokens, tokens), 0)
    token_at = lax.broadcasted_iota(jnp.int32, (tokens, tokens), 1)
    allowed = (seg_row == seg_row.T) & (key_at <= token_at)
    bias[...] = jnp.where(allowed, 0.0, -1e30)
    mid = tokens // 2

    def conv_head(g, j):
        cols = pl.ds(pl.multiple_of(g * width + j * HD, HD), HD)
        key = ck_s[:, g * HD : (g + 1) * HD]
        value = cv_s[:, g * HD : (g + 1) * HD]
        q, og = q_s[:, cols], og_s[:, cols]
        x0 = dot_nt(key[:mid], q) * factor + bias[:mid, :]
        x1 = dot_nt(key[mid:], q[mid:]) * factor + bias[mid:, mid:]
        d0 = dot_nt(value[:mid], og)
        d1 = dot_nt(value[mid:], og[mid:])
        top0 = jnp.max(x0, axis=0, keepdims=True)
        top1 = jnp.max(x1, axis=0, keepdims=True)
        top = jnp.concatenate([top0[:, :mid], jnp.maximum(top0[:, mid:], top1)], axis=1)
        e0 = jnp.exp2(x0 - top)
        e1 = jnp.exp2(x1 - top[:, mid:])
        l0 = jnp.sum(e0, axis=0, keepdims=True)
        l1 = jnp.sum(e1, axis=0, keepdims=True)
        a0 = jnp.sum(e0 * d0, axis=0, keepdims=True)
        a1 = jnp.sum(e1 * d1, axis=0, keepdims=True)
        h = g * heads + j
        stats[h, 0:1, :] = top
        stats[h, 1:2, :] = jnp.concatenate([l0[:, :mid], l0[:, mid:] + l1], axis=1)
        stats[h, 2:3, :] = jnp.concatenate([a0[:, :mid], a0[:, mid:] + a1], axis=1)

    for g in range(groups):
        for copy in in_copies[g]:
            copy.wait()
        pl.loop(0, heads, unroll=2)(functools.partial(conv_head, g))
        if g == groups - 2 and half > 1:
            gather[0].wait_recv()
            forward[1].start()
    for i in range(2, half):
        gather[i - 1].wait_recv()
        forward[i].start()
    for copy in forward:
        copy.wait_recv()

    def cart_head(g, j):
        cols = pl.ds(pl.multiple_of(g * width + j * HD, HD), HD)
        key = buf[:, g].reshape(cart, HD)
        value = buf[:, groups + g].reshape(cart, HD)
        q, og = q_s[:, cols], og_s[:, cols]
        h = g * heads + j
        x = dot_nt(key, q) * factor
        d = dot_nt(value, og)
        top_conv = stats[h, 0:1, :]
        top = jnp.maximum(jnp.max(x, axis=0, keepdims=True), top_conv)
        shrink = jnp.exp2(top_conv - top)
        e = jnp.exp2(x - top)
        total = stats[h, 1:2, :] * shrink + jnp.sum(e, axis=0, keepdims=True)
        weighted = stats[h, 2:3, :] * shrink + jnp.sum(e * d, axis=0, keepdims=True)
        inverse = 1.0 / total
        delta = weighted * inverse
        probs = e * inverse
        dscore = probs * (d - delta)
        part[g, :, :, 0] += dot(dscore.astype(jnp.bfloat16), q).reshape(half, 2, rows, HD)
        part[g, :, :, 1] += dot(probs.astype(jnp.bfloat16), og).reshape(half, 2, rows, HD)

    part[...] = jnp.zeros_like(part)
    peers = [lax.rem(me + 2 * i, n) for i in range(half)]
    pair_copies, place_copies, all_copies = [], [], []

    def start_pair(g):
        copy = remote(
            part.at[g, :, 1 - core], r1.at[g], s1_send.at[g], s1_recv.at[g], (dp, sibling)
        )
        copy.start()
        pair_copies.append(copy)

    def start_place(g):
        pair_copies[g].wait_recv()
        copies = []
        for i in range(1, half):
            to = lax.rem(place + i, half)
            s2[g, i] = (part[g, to, core] + r1[g, to]).astype(jnp.bfloat16)
            copy = remote(
                s2.at[g, i], r2.at[g, i], s2_send.at[g, i], s2_recv.at[g, i], (dp, peers[i])
            )
            copy.start()
            copies.append(copy)
        place_copies.append(copies)

    def start_all(g):
        total = part[g, place, core] + r1[g, place]
        for i in range(1, half):
            place_copies[g][i - 1].wait_recv()
            total = total + r2[g, i].astype(jnp.float32)
        r3[g, dp] = total.astype(jnp.bfloat16)
        copies = []
        for i in range(1, nd):
            copy = remote(
                r3.at[g, dp], r3.at[g, dp], s3_send.at[g, i], s3_recv.at[g, i],
                (lax.rem(dp + i, nd), me),
            )
            copy.start()
            copies.append(copy)
        all_copies.append(copies)

    def finish(g):
        for copy in all_copies[g]:
            copy.wait_recv()
        total = r3[g, 0].astype(jnp.float32)
        for i in range(1, nd):
            total = total + r3[g, i].astype(jnp.float32)
        dk_ref[:, g * HD : (g + 1) * HD] = total[0] * scale
        dv_ref[:, g * HD : (g + 1) * HD] = total[1]

    for g in range(groups):
        pl.loop(0, heads, unroll=2)(functools.partial(cart_head, g))
        start_pair(g)
        if g >= 1:
            start_place(g - 1)
        if g >= 2:
            start_all(g - 2)
    start_place(groups - 1)
    if groups > 1:
        start_all(groups - 2)
    for g in range(groups - 1):
        finish(g)
    start_all(groups - 1)
    finish(groups - 1)

    for copy in gather + forward + pair_copies:
        copy.wait_send()
    for copies in place_copies + all_copies:
        for copy in copies:
            copy.wait_send()


def solution(mesh):
    n, nd = mesh.shape["ctx"], mesh.shape["dp"]

    def per_device(queries, conv_keys, conv_values, out_grad, segment_ids, cart_keys, cart_values):
        tokens = queries.shape[0]
        rows = cart_keys.shape[0]
        groups = cart_keys.shape[1] // HD
        heads = queries.shape[1] // (groups * HD)
        half = n // 2
        bf16, f32 = jnp.bfloat16, jnp.float32
        dma = pltpu.SemaphoreType.DMA
        scratch = [
            pltpu.VMEM(queries.shape, bf16),
            pltpu.VMEM(out_grad.shape, bf16),
            pltpu.VMEM(conv_keys.shape, bf16),
            pltpu.VMEM(conv_values.shape, bf16),
            pltpu.VMEM(segment_ids.shape, jnp.int32),
            pltpu.VMEM((tokens, tokens), f32),
            pltpu.VMEM((groups * heads, 8, tokens), f32),
            pltpu.VMEM((n, 2 * groups, rows, HD), bf16),
            pltpu.VMEM((groups, half, 2, 2, rows, HD), f32),
            pltpu.VMEM((groups, half, 2, rows, HD), f32),
            pltpu.VMEM((groups, half, 2, rows, HD), bf16),
            pltpu.VMEM((groups, half, 2, rows, HD), bf16),
            pltpu.VMEM((groups, nd, 2, rows, HD), bf16),
            dma((2, groups)),
            dma((3,)),
            dma((2 * groups,)),
            dma((half,)),
            dma((half,)),
            dma((half,)),
            dma((half,)),
            dma((groups,)),
            dma((groups,)),
            dma((groups, half)),
            dma((groups, half)),
            dma((groups, nd)),
            dma((groups, nd)),
        ]
        return pl.pallas_call(
            functools.partial(kernel, n, nd, groups, heads),
            out_shape=[jax.ShapeDtypeStruct(cart_keys.shape, f32)] * 2,
            in_specs=[pl.BlockSpec(memory_space=pl.ANY)] * 7,
            out_specs=[pl.BlockSpec(memory_space=pltpu.VMEM)] * 2,
            scratch_shapes=scratch,
            compiler_params=pltpu.CompilerParams(
                collective_id=0, has_side_effects=True, vmem_limit_bytes=48 * 1024 * 1024
            ),
        )(queries, conv_keys, conv_values, out_grad, segment_ids, cart_keys, cart_values)

    in_specs = (P(("dp", "ctx"), None),) * 5 + (P("ctx", None),) * 2
    out_specs = (P("ctx", None), P("ctx", None))
    return jax.shard_map(
        per_device, mesh=mesh, in_specs=in_specs, out_specs=out_specs, check_vma=False
    )
```

```python
import functools
import math

import jax
import jax.numpy as jnp
from jax import lax
from jax.experimental import pallas as pl
from jax.experimental.pallas import tpu as pltpu
from jax.sharding import PartitionSpec as P

HD = 128
MESH = pl.DeviceIdType.MESH
NT = (((1,), (1,)), ((), ()))


def dot_nt(a, b):
    return lax.dot_general(a, b, NT, preferred_element_type=jnp.float32)


def dot(a, b):
    return jnp.dot(a, b, preferred_element_type=jnp.float32)


def kernel(
    n, nd, groups, heads,
    q_hbm, ck_hbm, cv_hbm, og_hbm, seg_hbm, kk_hbm, kv_hbm,
    dk_ref, dv_ref,
    q_s, og_s, ck_s, cv_s, seg_s, bias, stats, buf, part, r1, s2, r2, r3,
    score_a, score_b, dprob_a, dprob_b, tops_a, tops_b, probs_a, probs_b, dscore_a, dscore_b,
    in_sem, conv_sem, cart_sem,
    g_send, g_recv, f_send, f_recv, s1_send, s1_recv, s2_send, s2_recv, s3_send, s3_recv,
):
    dp, me = lax.axis_index("dp"), lax.axis_index("ctx")
    half = n // 2
    core = lax.rem(me, 2)
    place = me // 2
    sibling = me + 1 - 2 * core
    tokens = q_s.shape[0]
    rows = buf.shape[2]
    cart = n * rows
    width = heads * HD
    scale = 1.0 / math.sqrt(HD)
    factor = scale * math.log2(math.e)

    score, dprob, tops = (score_a, score_b), (dprob_a, dprob_b), (tops_a, tops_b)
    probs, dscore = (probs_a, probs_b), (dscore_a, dscore_b)

    barrier = pltpu.get_barrier_semaphore()
    pl.semaphore_signal(barrier, inc=1, device_id=(dp, sibling), device_id_type=MESH)
    for i in range(1, half):
        pl.semaphore_signal(
            barrier, inc=1, device_id=(dp, lax.rem(me + 2 * i, n)), device_id_type=MESH
        )
    for i in range(1, nd):
        pl.semaphore_signal(
            barrier, inc=1, device_id=(lax.rem(dp + i, nd), me), device_id_type=MESH
        )

    cart_copies = []
    for g in range(groups):
        cols = pl.ds(g * HD, HD)
        cart_copies.append(
            pltpu.make_async_copy(kk_hbm.at[:, cols], buf.at[me, g], cart_sem.at[g])
        )
        cart_copies.append(
            pltpu.make_async_copy(
                kv_hbm.at[:, cols], buf.at[me, groups + g], cart_sem.at[groups + g]
            )
        )
    for copy in cart_copies:
        copy.start()
    conv_copies = [
        pltpu.make_async_copy(seg_hbm, seg_s, conv_sem.at[0]),
        pltpu.make_async_copy(ck_hbm, ck_s, conv_sem.at[1]),
        pltpu.make_async_copy(cv_hbm, cv_s, conv_sem.at[2]),
    ]
    for copy in conv_copies:
        copy.start()

    def in_copies(g):
        cols = pl.ds(pl.multiple_of(g * width, width), width)
        return [
            pltpu.make_async_copy(q_hbm.at[:, cols], q_s.at[:, cols], in_sem.at[0, g]),
            pltpu.make_async_copy(og_hbm.at[:, cols], og_s.at[:, cols], in_sem.at[1, g]),
        ]

    for g in range(groups):
        for copy in in_copies(g):
            copy.start()
    for copy in cart_copies:
        copy.wait()
    pl.semaphore_wait(barrier, 1 + (half - 1) + (nd - 1))

    def remote(src, dst, send, recv, target):
        return pltpu.make_async_remote_copy(
            src_ref=src, dst_ref=dst, send_sem=send, recv_sem=recv,
            device_id=target, device_id_type=MESH,
        )

    gather = [
        remote(
            buf.at[me], buf.at[me], g_send.at[i], g_recv.at[i], (dp, lax.rem(me + 2 * i, n))
        )
        for i in range(1, half)
    ]
    arrivals = [lax.rem(me + n - 2 * i, n) for i in range(half)]
    forward = [
        remote(buf.at[a], buf.at[a], f_send.at[i], f_recv.at[i], (dp, sibling))
        for i, a in enumerate(arrivals)
    ]
    for copy in gather:
        copy.start()
    forward[0].start()

    for copy in conv_copies:
        copy.wait()
    seg_row = jnp.broadcast_to(seg_s[...].astype(jnp.float32), (tokens, tokens))
    key_at = lax.broadcasted_iota(jnp.int32, (tokens, tokens), 0)
    token_at = lax.broadcasted_iota(jnp.int32, (tokens, tokens), 1)
    allowed = (seg_row == seg_row.T) & (key_at <= token_at)
    bias[...] = jnp.where(allowed, 0.0, -1e30)
    mid = tokens // 2

    strip = 32

    def fold(x, reduce):
        return reduce(x.reshape(x.shape[0] // 8, 8, x.shape[1]), axis=0)

    def head_cols(g, j):
        return pl.ds(pl.multiple_of(g * width + j * HD, HD), HD)

    def conv_products(g, j, slot):
        cols, own = head_cols(g, j), pl.ds(pl.multiple_of(g * HD, HD), HD)
        q, og = q_s[:, cols], og_s[:, cols]
        s0 = dot_nt(ck_s[:mid, own], q) + bias[:mid, :]
        s1 = dot_nt(ck_s[mid:, own], q[mid:]) + bias[mid:, mid:]
        score[slot][:mid, :] = s0
        score[slot][mid:tokens, mid:] = s1
        dprob[slot][:mid, :] = dot_nt(cv_s[:mid, own], og)
        dprob[slot][mid:tokens, mid:] = dot_nt(cv_s[mid:, own], og[mid:])
        top0 = jnp.max(fold(s0, jnp.max), axis=0, keepdims=True)
        top1 = jnp.max(fold(s1, jnp.max), axis=0, keepdims=True)
        tops[slot][0:1, :] = jnp.concatenate(
            [top0[:, :mid], jnp.maximum(top0[:, mid:], top1)], axis=1
        ) * factor

    def conv_sums(g, j, slot):
        top = tops[slot][0:1, :]
        total = weighted = None
        for low in range(0, mid, strip):
            e = jnp.exp2(score[slot][low : low + strip, :] * factor - top)
            w = e * dprob[slot][low : low + strip, :]
            e, w = fold(e, jnp.sum), fold(w, jnp.sum)
            total, weighted = (e, w) if total is None else (total + e, weighted + w)
        late_total = late_weighted = None
        for low in range(mid, tokens, strip):
            e = jnp.exp2(score[slot][low : low + strip, mid:] * factor - top[:, mid:])
            w = e * dprob[slot][low : low + strip, mid:]
            e, w = fold(e, jnp.sum), fold(w, jnp.sum)
            late_total, late_weighted = (
                (e, w) if late_total is None else (late_total + e, late_weighted + w)
            )

        def whole(early, late):
            both = jnp.concatenate([early[:, :mid], early[:, mid:] + late], axis=1)
            return jnp.sum(both, axis=0, keepdims=True)

        h = g * heads + j
        stats[h, 0:1, :] = top
        stats[h, 1:2, :] = whole(total, late_total)
        stats[h, 2:3, :] = whole(weighted, late_weighted)

    def conv_group(g):
        for copy in in_copies(g):
            copy.wait()
        conv_products(g, 0, 0)
        for j in range(heads):
            if j + 1 < heads:
                conv_products(g, j + 1, (j + 1) % 2)
            conv_sums(g, j, j % 2)

        if half > 1:
            @pl.when(g == groups - 2)
            def _():
                gather[0].wait_recv()
                forward[1].start()

    pl.loop(0, groups)(conv_group)
    for i in range(2, half):
        gather[i - 1].wait_recv()
        forward[i].start()
    for copy in forward:
        copy.wait_recv()

    def cart_products(g, j, slot):
        cols = head_cols(g, j)
        s = dot_nt(buf[:, g].reshape(cart, HD), q_s[:, cols])
        score[slot][:cart, :] = s
        tops[slot][0:1, :] = jnp.max(fold(s, jnp.max), axis=0, keepdims=True) * factor
        dprob[slot][:cart, :] = dot_nt(buf[:, groups + g].reshape(cart, HD), og_s[:, cols])

    def cart_probs(g, j, slot):
        h = g * heads + j
        top_conv = stats[h, 0:1, :]
        top = jnp.maximum(tops[slot][0:1, :], top_conv)
        total = weighted = None
        for low in range(0, cart, strip):
            e = jnp.exp2(score[slot][low : low + strip, :] * factor - top)
            score[slot][low : low + strip, :] = e
            w = e * dprob[slot][low : low + strip, :]
            e, w = fold(e, jnp.sum), fold(w, jnp.sum)
            total, weighted = (e, w) if total is None else (total + e, weighted + w)
        shrink = jnp.exp2(top_conv - top)
        total = stats[h, 1:2, :] * shrink + jnp.sum(total, axis=0, keepdims=True)
        weighted = stats[h, 2:3, :] * shrink + jnp.sum(weighted, axis=0, keepdims=True)
        inverse = 1.0 / total
        delta = weighted * inverse
        for low in range(0, cart, strip):
            p = score[slot][low : low + strip, :] * inverse
            probs[slot][low : low + strip, :] = p.astype(jnp.bfloat16)
            ds = p * (dprob[slot][low : low + strip, :] - delta)
            dscore[slot][low : low + strip, :] = ds.astype(jnp.bfloat16)

    def cart_grads(g, j, slot):
        cols = head_cols(g, j)
        for kind, (left, right) in enumerate(((dscore, q_s), (probs, og_s))):
            term = dot(left[slot][...], right[:, cols]).reshape(half, 2, rows, HD)
            if j > 0:
                term = part[g, :, :, kind] + term
            part[g, :, :, kind] = term

    peers = [lax.rem(me + 2 * i, n) for i in range(half)]
    def pair_copy(g):
        return remote(
            part.at[g, :, 1 - core], r1.at[g], s1_send.at[g], s1_recv.at[g], (dp, sibling)
        )

    def place_copy(g, i):
        return remote(
            s2.at[g, i], r2.at[g, i], s2_send.at[g, i], s2_recv.at[g, i], (dp, peers[i])
        )

    def all_copy(g, i):
        return remote(
            r3.at[g, dp], r3.at[g, dp], s3_send.at[g, i], s3_recv.at[g, i],
            (lax.rem(dp + i, nd), me),
        )

    def start_place(g):
        pair_copy(g).wait_recv()
        for i in range(1, half):
            to = lax.rem(place + i, half)
            s2[g, i] = (part[g, to, core] + r1[g, to]).astype(jnp.bfloat16)
            place_copy(g, i).start()

    def start_all(g):
        total = part[g, place, core] + r1[g, place]
        for i in range(1, half):
            place_copy(g, i).wait_recv()
            total = total + r2[g, i].astype(jnp.float32)
        r3[g, dp] = total.astype(jnp.bfloat16)
        for i in range(1, nd):
            all_copy(g, i).start()

    def finish(g):
        for i in range(1, nd):
            all_copy(g, i).wait_recv()
        total = r3[g, 0].astype(jnp.float32)
        for i in range(1, nd):
            total = total + r3[g, i].astype(jnp.float32)
        dk_ref[:, g * HD : (g + 1) * HD] = total[0] * scale
        dv_ref[:, g * HD : (g + 1) * HD] = total[1]

    def cart_group(g):
        cart_products(g, 0, 0)
        for j in range(heads):
            if j + 1 < heads:
                cart_products(g, j + 1, (j + 1) % 2)
            cart_probs(g, j, j % 2)
            cart_grads(g, j, j % 2)
        pair_copy(g).start()

        @pl.when(g >= 1)
        def _():
            start_place(g - 1)

        @pl.when(g >= 2)
        def _():
            start_all(g - 2)

    pl.loop(0, groups)(cart_group)
    start_place(groups - 1)
    if groups > 1:
        start_all(groups - 2)
    for g in range(groups - 1):
        finish(g)
    start_all(groups - 1)
    finish(groups - 1)

    for copy in gather + forward:
        copy.wait_send()
    for g in range(groups):
        pair_copy(g).wait_send()
        for i in range(1, half):
            place_copy(g, i).wait_send()
        for i in range(1, nd):
            all_copy(g, i).wait_send()


def solution(mesh):
    n, nd = mesh.shape["ctx"], mesh.shape["dp"]

    def per_device(queries, conv_keys, conv_values, out_grad, segment_ids, cart_keys, cart_values):
        tokens = queries.shape[0]
        rows = cart_keys.shape[0]
        groups = cart_keys.shape[1] // HD
        heads = queries.shape[1] // (groups * HD)
        half = n // 2
        bf16, f32 = jnp.bfloat16, jnp.float32
        dma = pltpu.SemaphoreType.DMA
        scratch = [
            pltpu.VMEM(queries.shape, bf16),
            pltpu.VMEM(out_grad.shape, bf16),
            pltpu.VMEM(conv_keys.shape, bf16),
            pltpu.VMEM(conv_values.shape, bf16),
            pltpu.VMEM(segment_ids.shape, jnp.int32),
            pltpu.VMEM((tokens, tokens), f32),
            pltpu.VMEM((groups * heads, 8, tokens), f32),
            pltpu.VMEM((n, 2 * groups, rows, HD), bf16),
            pltpu.VMEM((groups, half, 2, 2, rows, HD), f32),
            pltpu.VMEM((groups, half, 2, rows, HD), f32),
            pltpu.VMEM((groups, half, 2, rows, HD), bf16),
            pltpu.VMEM((groups, half, 2, rows, HD), bf16),
            pltpu.VMEM((groups, nd, 2, rows, HD), bf16),
            *[pltpu.VMEM((max(n * rows, tokens), tokens), f32)] * 4,
            *[pltpu.VMEM((8, tokens), f32)] * 2,
            *[pltpu.VMEM((n * rows, tokens), bf16)] * 4,
            dma((2, groups)),
            dma((3,)),
            dma((2 * groups,)),
            dma((half,)),
            dma((half,)),
            dma((half,)),
            dma((half,)),
            dma((groups,)),
            dma((groups,)),
            dma((groups, half)),
            dma((groups, half)),
            dma((groups, nd)),
            dma((groups, nd)),
        ]
        return pl.pallas_call(
            functools.partial(kernel, n, nd, groups, heads),
            out_shape=[jax.ShapeDtypeStruct(cart_keys.shape, f32)] * 2,
            in_specs=[pl.BlockSpec(memory_space=pltpu.HBM)] * 7,
            out_specs=[pl.BlockSpec(memory_space=pltpu.VMEM)] * 2,
            scratch_shapes=scratch,
            compiler_params=pltpu.CompilerParams(
                collective_id=0, has_side_effects=True, vmem_limit_bytes=64 * 1024 * 1024
            ),
        )(queries, conv_keys, conv_values, out_grad, segment_ids, cart_keys, cart_values)

    in_specs = (P(("dp", "ctx"), None),) * 5 + (P("ctx", None),) * 2
    out_specs = (P("ctx", None), P("ctx", None))
    return jax.shard_map(
        per_device, mesh=mesh, in_specs=in_specs, out_specs=out_specs, check_vma=False
    )
```

```python
import functools
import math

import jax
import jax.numpy as jnp
from jax import lax
from jax.experimental import pallas as pl
from jax.experimental.pallas import tpu as pltpu
from jax.sharding import PartitionSpec as P

HD = 128
MESH = pl.DeviceIdType.MESH
NT = (((1,), (1,)), ((), ()))


def dot_nt(a, b):
    return lax.dot_general(a, b, NT, preferred_element_type=jnp.float32)


def dot(a, b):
    return jnp.dot(a, b, preferred_element_type=jnp.float32)


def kernel(
    n, nd, groups, heads,
    q_hbm, ck_hbm, cv_hbm, og_hbm, seg_hbm, kk_hbm, kv_hbm,
    out_ref,
    q_s, og_s, ck_s, cv_s, seg_s, bias, stats, buf, part, r1, s2, r2, r3,
    score_a, score_b, dprob_a, dprob_b, tops_a, tops_b, probs_a, probs_b, dscore_a, dscore_b,
    in_sem, conv_sem, cart_sem,
    g_send, g_recv, f_send, f_recv, s1_send, s1_recv, s2_send, s2_recv, s3_send, s3_recv,
):
    dp, me = lax.axis_index("dp"), lax.axis_index("ctx")
    half = n // 2
    core = lax.rem(me, 2)
    place = me // 2
    sibling = me + 1 - 2 * core
    tokens = q_s.shape[0]
    rows = buf.shape[3]
    cart = n * rows
    width = heads * HD
    factor = math.log2(math.e) / math.sqrt(HD)

    score, dprob, tops = (score_a, score_b), (dprob_a, dprob_b), (tops_a, tops_b)
    probs, dscore = (probs_a, probs_b), (dscore_a, dscore_b)

    barrier = pltpu.get_barrier_semaphore()
    pl.semaphore_signal(barrier, inc=1, device_id=(dp, sibling), device_id_type=MESH)
    for i in range(1, half):
        pl.semaphore_signal(
            barrier, inc=1, device_id=(dp, lax.rem(me + 2 * i, n)), device_id_type=MESH
        )
    for i in range(1, nd):
        pl.semaphore_signal(
            barrier, inc=1, device_id=(lax.rem(dp + i, nd), me), device_id_type=MESH
        )

    cart_copies = []
    for g in range(groups):
        cols = pl.ds(g * HD, HD)
        for kind, ref in enumerate((kk_hbm, kv_hbm)):
            cart_copies.append(
                pltpu.make_async_copy(
                    ref.at[:, cols], buf.at[g, me, kind], cart_sem.at[kind, g]
                )
            )
    for copy in cart_copies:
        copy.start()
    conv_copies = [
        pltpu.make_async_copy(seg_hbm, seg_s, conv_sem.at[0]),
        pltpu.make_async_copy(ck_hbm, ck_s, conv_sem.at[1]),
        pltpu.make_async_copy(cv_hbm, cv_s, conv_sem.at[2]),
    ]
    for copy in conv_copies:
        copy.start()

    def in_copies(g):
        cols = pl.ds(pl.multiple_of(g * width, width), width)
        return [
            pltpu.make_async_copy(q_hbm.at[:, cols], q_s.at[:, cols], in_sem.at[0, g]),
            pltpu.make_async_copy(og_hbm.at[:, cols], og_s.at[:, cols], in_sem.at[1, g]),
        ]

    for g in range(groups):
        for copy in in_copies(g):
            copy.start()
    for copy in cart_copies:
        copy.wait()
    pl.semaphore_wait(barrier, 1 + (half - 1) + (nd - 1))

    def remote(src, dst, send, recv, target):
        return pltpu.make_async_remote_copy(
            src_ref=src, dst_ref=dst, send_sem=send, recv_sem=recv,
            device_id=target, device_id_type=MESH,
        )

    def gather(g, i):
        return remote(
            buf.at[g, me], buf.at[g, me], g_send.at[g, i], g_recv.at[g, i],
            (dp, lax.rem(me + 2 * i, n)),
        )

    def forward(g, i):
        chunk = buf.at[g, lax.rem(me + n - 2 * i, n)]
        return remote(chunk, chunk, f_send.at[g, i], f_recv.at[g, i], (dp, sibling))

    def pass_on(g):
        for i in range(1, half):
            gather(g, i).wait_recv()
            forward(g, i).start()

    def gathered(g):
        for i in range(half):
            forward(g, i).wait_recv()

    for g in range(groups):
        for i in range(1, half):
            gather(g, i).start()
        forward(g, 0).start()

    for copy in conv_copies:
        copy.wait()
    seg_row = jnp.broadcast_to(seg_s[...].astype(jnp.float32), (tokens, tokens))
    key_at = lax.broadcasted_iota(jnp.int32, (tokens, tokens), 0)
    token_at = lax.broadcasted_iota(jnp.int32, (tokens, tokens), 1)
    allowed = (seg_row == seg_row.T) & (key_at <= token_at)
    bias[...] = jnp.where(allowed, 0.0, -1e30)
    mid = tokens // 2

    strip = 32

    def fold(x, reduce):
        return reduce(x.reshape(x.shape[0] // 8, 8, x.shape[1]), axis=0)

    def head_cols(g, j):
        return pl.ds(pl.multiple_of(g * width + j * HD, HD), HD)

    def conv_products(g, j, slot):
        cols, own = head_cols(g, j), pl.ds(pl.multiple_of(g * HD, HD), HD)
        q, og = q_s[:, cols], og_s[:, cols]
        s0 = dot_nt(ck_s[:mid, own], q) + bias[:mid, :]
        s1 = dot_nt(ck_s[mid:, own], q[mid:]) + bias[mid:, mid:]
        score[slot][:mid, :] = s0
        score[slot][mid:tokens, mid:] = s1
        dprob[slot][:mid, :] = dot_nt(cv_s[:mid, own], og)
        dprob[slot][mid:tokens, mid:] = dot_nt(cv_s[mid:, own], og[mid:])
        top0 = jnp.max(fold(s0, jnp.max), axis=0, keepdims=True)
        top1 = jnp.max(fold(s1, jnp.max), axis=0, keepdims=True)
        tops[slot][0:1, :] = jnp.concatenate(
            [top0[:, :mid], jnp.maximum(top0[:, mid:], top1)], axis=1
        ) * factor

    def conv_sums(g, j, slot):
        top = tops[slot][0:1, :]
        total = weighted = None
        for low in range(0, mid, strip):
            e = jnp.exp2(score[slot][low : low + strip, :] * factor - top)
            w = e * dprob[slot][low : low + strip, :]
            e, w = fold(e, jnp.sum), fold(w, jnp.sum)
            total, weighted = (e, w) if total is None else (total + e, weighted + w)
        late_total = late_weighted = None
        for low in range(mid, tokens, strip):
            e = jnp.exp2(score[slot][low : low + strip, mid:] * factor - top[:, mid:])
            w = e * dprob[slot][low : low + strip, mid:]
            e, w = fold(e, jnp.sum), fold(w, jnp.sum)
            late_total, late_weighted = (
                (e, w) if late_total is None else (late_total + e, late_weighted + w)
            )

        def whole(early, late):
            both = jnp.concatenate([early[:, :mid], early[:, mid:] + late], axis=1)
            return jnp.sum(both, axis=0, keepdims=True)

        h = g * heads + j
        stats[h, 0:1, :] = top
        stats[h, 1:2, :] = whole(total, late_total)
        stats[h, 2:3, :] = whole(weighted, late_weighted)

    per = heads // 2

    def next_of(step, j):
        head = jnp.minimum(step * per + j + 1, groups * heads - 1)
        return head // heads, lax.rem(head, heads)

    def conv_step(step):
        g, first = step // 2, lax.rem(step, 2) * per

        @pl.when((first > 0) & (g + 1 < groups))
        def _():
            for copy in in_copies(g + 1):
                copy.wait()

        for j in range(per):
            conv_products(*next_of(step, j), (j + 1) % 2)
            conv_sums(g, first + j, j % 2)

        @pl.when((first > 0) & (g >= 1))
        def _():
            pass_on(g - 1)

    for copy in in_copies(0):
        copy.wait()
    conv_products(0, 0, 0)
    pl.loop(0, 2 * groups)(conv_step)
    pass_on(groups - 1)

    def cart_products(g, j, slot):
        cols = head_cols(g, j)
        s = dot_nt(buf[g, :, 0].reshape(cart, HD), q_s[:, cols])
        score[slot][:cart, :] = s
        tops[slot][0:1, :] = jnp.max(fold(s, jnp.max), axis=0, keepdims=True) * factor
        dprob[slot][:cart, :] = dot_nt(buf[g, :, 1].reshape(cart, HD), og_s[:, cols])

    def cart_probs(g, j, slot):
        h = g * heads + j
        top_conv = stats[h, 0:1, :]
        top = jnp.maximum(tops[slot][0:1, :], top_conv)
        total = weighted = None
        for low in range(0, cart, strip):
            e = jnp.exp2(score[slot][low : low + strip, :] * factor - top)
            score[slot][low : low + strip, :] = e
            w = e * dprob[slot][low : low + strip, :]
            e, w = fold(e, jnp.sum), fold(w, jnp.sum)
            total, weighted = (e, w) if total is None else (total + e, weighted + w)
        shrink = jnp.exp2(top_conv - top)
        total = stats[h, 1:2, :] * shrink + jnp.sum(total, axis=0, keepdims=True)
        weighted = stats[h, 2:3, :] * shrink + jnp.sum(weighted, axis=0, keepdims=True)
        inverse = 1.0 / total
        delta = weighted * inverse
        for low in range(0, cart, strip):
            p = score[slot][low : low + strip, :] * inverse
            probs[slot][low : low + strip, :] = p.astype(jnp.bfloat16)
            ds = p * (dprob[slot][low : low + strip, :] - delta)
            dscore[slot][low : low + strip, :] = ds.astype(jnp.bfloat16)

    def cart_grads(g, j, slot):
        cols = head_cols(g, j)
        for kind, (left, right) in enumerate(((dscore, q_s), (probs, og_s))):
            term = dot(left[slot][...], right[:, cols]).reshape(half, 2, rows, HD)
            part[g, :, :, kind] += term

    part[...] = jnp.zeros_like(part)
    peers = [lax.rem(me + 2 * i, n) for i in range(half)]
    def pair_copy(g):
        return remote(
            part.at[g, :, 1 - core], r1.at[g], s1_send.at[g], s1_recv.at[g], (dp, sibling)
        )

    def place_copy(g, i):
        return remote(
            s2.at[g, i], r2.at[g, i], s2_send.at[g, i], s2_recv.at[g, i], (dp, peers[i])
        )

    def all_copy(g, i):
        return remote(
            r3.at[g, dp], r3.at[g, dp], s3_send.at[g, i], s3_recv.at[g, i],
            (lax.rem(dp + i, nd), me),
        )

    def start_place(g):
        pair_copy(g).wait_recv()
        for i in range(1, half):
            to = lax.rem(place + i, half)
            s2[g, i] = (part[g, to, core] + r1[g, to]).astype(jnp.bfloat16)
            place_copy(g, i).start()

    def start_all(g):
        total = part[g, place, core] + r1[g, place]
        for i in range(1, half):
            place_copy(g, i).wait_recv()
            total = total + r2[g, i].astype(jnp.float32)
        r3[g, dp] = total.astype(jnp.bfloat16)
        for i in range(1, nd):
            all_copy(g, i).start()

    def finish(g):
        for i in range(1, nd):
            all_copy(g, i).wait_recv()
        total = r3[g, 0].astype(jnp.float32)
        for i in range(1, nd):
            total = total + r3[g, i].astype(jnp.float32)
        out_ref[:, :, g * HD : (g + 1) * HD] = total

    def cart_step(step):
        g, first = step // 2, lax.rem(step, 2) * per

        @pl.when((first > 0) & (g + 1 < groups))
        def _():
            gathered(g + 1)

        for j in range(per):
            cart_products(*next_of(step, j), (j + 1) % 2)
            cart_probs(g, first + j, j % 2)
            cart_grads(g, first + j, j % 2)

        @pl.when(first > 0)
        def _():
            pair_copy(g).start()

        @pl.when((first == 0) & (g >= 1))
        def _():
            start_place(g - 1)

        @pl.when((first == 0) & (g >= 2))
        def _():
            start_all(g - 2)

    gathered(0)
    cart_products(0, 0, 0)
    pl.loop(0, 2 * groups)(cart_step)
    start_place(groups - 1)
    if groups > 1:
        start_all(groups - 2)
    for g in range(groups - 1):
        finish(g)
    start_all(groups - 1)
    finish(groups - 1)

    for g in range(groups):
        for i in range(1, half):
            gather(g, i).wait_send()
        for i in range(half):
            forward(g, i).wait_send()
        pair_copy(g).wait_send()
        for i in range(1, half):
            place_copy(g, i).wait_send()
        for i in range(1, nd):
            all_copy(g, i).wait_send()


def solution(mesh):
    n, nd = mesh.shape["ctx"], mesh.shape["dp"]

    def per_device(queries, conv_keys, conv_values, out_grad, segment_ids, cart_keys, cart_values):
        tokens = queries.shape[0]
        rows = cart_keys.shape[0]
        groups = cart_keys.shape[1] // HD
        heads = queries.shape[1] // (groups * HD)
        half = n // 2
        bf16, f32 = jnp.bfloat16, jnp.float32
        dma = pltpu.SemaphoreType.DMA
        scratch = [
            pltpu.VMEM(queries.shape, bf16),
            pltpu.VMEM(out_grad.shape, bf16),
            pltpu.VMEM(conv_keys.shape, bf16),
            pltpu.VMEM(conv_values.shape, bf16),
            pltpu.VMEM(segment_ids.shape, jnp.int32),
            pltpu.VMEM((tokens, tokens), f32),
            pltpu.VMEM((groups * heads, 8, tokens), f32),
            pltpu.VMEM((groups, n, 2, rows, HD), bf16),
            pltpu.VMEM((groups, half, 2, 2, rows, HD), f32),
            pltpu.VMEM((groups, half, 2, rows, HD), f32),
            pltpu.VMEM((groups, half, 2, rows, HD), bf16),
            pltpu.VMEM((groups, half, 2, rows, HD), bf16),
            pltpu.VMEM((groups, nd, 2, rows, HD), bf16),
            *[pltpu.VMEM((max(n * rows, tokens), tokens), f32)] * 4,
            *[pltpu.VMEM((8, tokens), f32)] * 2,
            *[pltpu.VMEM((n * rows, tokens), bf16)] * 4,
            dma((2, groups)),
            dma((3,)),
            dma((2, groups)),
            *[dma((groups, half))] * 4,
            dma((groups,)),
            dma((groups,)),
            dma((groups, half)),
            dma((groups, half)),
            dma((groups, nd)),
            dma((groups, nd)),
        ]
        out = pl.pallas_call(
            functools.partial(kernel, n, nd, groups, heads),
            out_shape=jax.ShapeDtypeStruct((2, *cart_keys.shape), f32),
            in_specs=[pl.BlockSpec(memory_space=pltpu.HBM)] * 7,
            out_specs=pl.BlockSpec(memory_space=pltpu.VMEM),
            scratch_shapes=scratch,
            compiler_params=pltpu.CompilerParams(
                collective_id=0, has_side_effects=True, vmem_limit_bytes=64 * 1024 * 1024
            ),
        )(queries, conv_keys, conv_values, out_grad, segment_ids, cart_keys, cart_values)
        return out[0] * (1.0 / math.sqrt(HD)), out[1]

    in_specs = (P(("dp", "ctx"), None),) * 5 + (P("ctx", None),) * 2
    out_specs = (P("ctx", None), P("ctx", None))
    return jax.shard_map(
        per_device, mesh=mesh, in_specs=in_specs, out_specs=out_specs, check_vma=False
    )
```

```python
import functools
import math

import jax
import jax.numpy as jnp
from jax import lax
from jax.experimental import pallas as pl
from jax.experimental.pallas import tpu as pltpu
from jax.sharding import PartitionSpec as P

HD = 128
MESH = pl.DeviceIdType.MESH
NT = (((1,), (1,)), ((), ()))


def dot_nt(a, b):
    return lax.dot_general(a, b, NT, preferred_element_type=jnp.float32)


def dot(a, b):
    return jnp.dot(a, b, preferred_element_type=jnp.float32)


def kernel(
    n, nd, groups, heads,
    q_hbm, ck_hbm, cv_hbm, og_hbm, seg_hbm, kk_hbm, kv_hbm,
    out_ref,
    q_s, og_s, ck_s, cv_s, seg_s, bias, stats, buf, part, r1, s2, r2, r3,
    score_a, score_b, dprob_a, dprob_b, tops_a, tops_b, probs_a, probs_b, dscore_a, dscore_b,
    in_sem, conv_sem, cart_sem,
    g_send, g_recv, f_send, f_recv, s1_send, s1_recv, s2_send, s2_recv, s3_send, s3_recv,
):
    dp, me = lax.axis_index("dp"), lax.axis_index("ctx")
    half = n // 2
    core = lax.rem(me, 2)
    place = me // 2
    sibling = me + 1 - 2 * core
    tokens = q_s.shape[0]
    rows = buf.shape[3]
    cart = n * rows
    width = heads * HD
    factor = math.log2(math.e) / math.sqrt(HD)

    score, dprob, tops = (score_a, score_b), (dprob_a, dprob_b), (tops_a, tops_b)
    probs, dscore = (probs_a, probs_b), (dscore_a, dscore_b)

    barrier = pltpu.get_barrier_semaphore()
    pl.semaphore_signal(barrier, inc=1, device_id=(dp, sibling), device_id_type=MESH)
    for i in range(1, half):
        pl.semaphore_signal(
            barrier, inc=1, device_id=(dp, lax.rem(me + 2 * i, n)), device_id_type=MESH
        )
    for i in range(1, nd):
        pl.semaphore_signal(
            barrier, inc=1, device_id=(lax.rem(dp + i, nd), me), device_id_type=MESH
        )

    cart_copies = []
    for g in range(groups):
        cols = pl.ds(g * HD, HD)
        for kind, ref in enumerate((kk_hbm, kv_hbm)):
            cart_copies.append(
                pltpu.make_async_copy(
                    ref.at[:, cols], buf.at[g, me, kind], cart_sem.at[kind, g]
                )
            )
    for copy in cart_copies:
        copy.start()
    conv_copies = [
        pltpu.make_async_copy(seg_hbm, seg_s, conv_sem.at[0]),
        pltpu.make_async_copy(ck_hbm, ck_s, conv_sem.at[1]),
        pltpu.make_async_copy(cv_hbm, cv_s, conv_sem.at[2]),
    ]
    for copy in conv_copies:
        copy.start()

    def in_copies(g):
        cols = pl.ds(pl.multiple_of(g * width, width), width)
        return [
            pltpu.make_async_copy(q_hbm.at[:, cols], q_s.at[:, cols], in_sem.at[0, g]),
            pltpu.make_async_copy(og_hbm.at[:, cols], og_s.at[:, cols], in_sem.at[1, g]),
        ]

    for g in range(groups):
        for copy in in_copies(g):
            copy.start()
    for copy in cart_copies:
        copy.wait()
    pl.semaphore_wait(barrier, 1 + (half - 1) + (nd - 1))

    def remote(src, dst, send, recv, target):
        return pltpu.make_async_remote_copy(
            src_ref=src, dst_ref=dst, send_sem=send, recv_sem=recv,
            device_id=target, device_id_type=MESH,
        )

    def gather(g, i):
        return remote(
            buf.at[g, me], buf.at[g, me], g_send.at[g, i], g_recv.at[g, i],
            (dp, lax.rem(me + 2 * i, n)),
        )

    def forward(g, i):
        chunk = buf.at[g, lax.rem(me + n - 2 * i, n)]
        return remote(chunk, chunk, f_send.at[g, i], f_recv.at[g, i], (dp, sibling))

    def pass_on(g):
        for i in range(1, half):
            gather(g, i).wait_recv()
            forward(g, i).start()

    def gathered(g):
        for i in range(half):
            forward(g, i).wait_recv()

    for g in range(groups):
        for i in range(1, half):
            gather(g, i).start()
        forward(g, 0).start()

    for copy in conv_copies:
        copy.wait()
    seg_row = jnp.broadcast_to(seg_s[...].astype(jnp.float32), (tokens, tokens))
    key_at = lax.broadcasted_iota(jnp.int32, (tokens, tokens), 0)
    token_at = lax.broadcasted_iota(jnp.int32, (tokens, tokens), 1)
    allowed = (seg_row == seg_row.T) & (key_at <= token_at)
    bias[...] = jnp.where(allowed, 0.0, -1e30)
    mid = tokens // 2

    strip = 32

    def fold(x, reduce):
        return reduce(x.reshape(x.shape[0] // 8, 8, x.shape[1]), axis=0)

    def head_cols(g, j):
        return pl.ds(pl.multiple_of(g * width + j * HD, HD), HD)

    pairs = groups * heads // 2

    def place_of(pair):
        head = jnp.clip(pair, 0, pairs - 1) * 2
        return head // heads, lax.rem(head, heads)

    def conv_products(pair, slot):
        g, j = place_of(pair)
        own = pl.ds(pl.multiple_of(g * HD, HD), HD)
        for u in range(2):
            q, og = q_s[:, head_cols(g, j + u)], og_s[:, head_cols(g, j + u)]
            s0 = dot_nt(ck_s[:mid, own], q) + bias[:mid, :]
            s1 = dot_nt(ck_s[mid:, own], q[mid:]) + bias[mid:, mid:]
            score[slot][u, :mid, :] = s0
            score[slot][u, mid:tokens, mid:] = s1
            dprob[slot][u, :mid, :] = dot_nt(cv_s[:mid, own], og)
            dprob[slot][u, mid:tokens, mid:] = dot_nt(cv_s[mid:, own], og[mid:])
            top0, top1 = fold(s0, jnp.max), fold(s1, jnp.max)
            top = jnp.concatenate([top0[:, :mid], jnp.maximum(top0[:, mid:], top1)], axis=1)
            tops[slot][u : u + 1, :] = jnp.max(top, axis=0, keepdims=True) * factor

    def conv_sums(pair, slot):
        for u in range(2):
            top = tops[slot][u : u + 1, :]
            total = weighted = None
            for low in range(0, mid, strip):
                e = jnp.exp2(score[slot][u, low : low + strip, :] * factor - top)
                w = e * dprob[slot][u, low : low + strip, :]
                e, w = fold(e, jnp.sum), fold(w, jnp.sum)
                total, weighted = (e, w) if total is None else (total + e, weighted + w)
            late_total = late_weighted = None
            for low in range(mid, tokens, strip):
                e = jnp.exp2(score[slot][u, low : low + strip, mid:] * factor - top[:, mid:])
                w = e * dprob[slot][u, low : low + strip, mid:]
                e, w = fold(e, jnp.sum), fold(w, jnp.sum)
                late_total, late_weighted = (
                    (e, w) if late_total is None else (late_total + e, late_weighted + w)
                )

            def whole(early, late):
                both = jnp.concatenate([early[:, :mid], early[:, mid:] + late], axis=1)
                return jnp.sum(both, axis=0, keepdims=True)

            stats[2 * pair + u, 0:1, :] = top
            stats[2 * pair + u, 1:2, :] = whole(total, late_total)
            stats[2 * pair + u, 2:3, :] = whole(weighted, late_weighted)

    def conv_step(step):
        g, late = step // 2, lax.rem(step, 2) == 1

        @pl.when(late & (g + 1 < groups))
        def _():
            for copy in in_copies(g + 1):
                copy.wait()

        for i in range(per):
            conv_products(step * per + i + 1, (i + 1) % 2)
            conv_sums(step * per + i, i % 2)

        @pl.when(late & (g >= 1))
        def _():
            pass_on(g - 1)

    per = heads // 4
    for copy in in_copies(0):
        copy.wait()
    conv_products(0, 0)
    pl.loop(0, 2 * groups)(conv_step)
    pass_on(groups - 1)

    def cart_products(pair, slot):
        g, j = place_of(pair)
        for u in range(2):
            cols = head_cols(g, j + u)
            s = dot_nt(buf[g, :, 0].reshape(cart, HD), q_s[:, cols])
            score[slot][u, :cart, :] = s
            tops[slot][u : u + 1, :] = jnp.max(fold(s, jnp.max), axis=0, keepdims=True) * factor
            dprob[slot][u, :cart, :] = dot_nt(buf[g, :, 1].reshape(cart, HD), og_s[:, cols])

    def cart_probs(pair, slot):
        for u in range(2):
            h = 2 * pair + u
            top_conv = stats[h, 0:1, :]
            top = jnp.maximum(tops[slot][u : u + 1, :], top_conv)
            total = weighted = None
            for low in range(0, cart, strip):
                e = jnp.exp2(score[slot][u, low : low + strip, :] * factor - top)
                score[slot][u, low : low + strip, :] = e
                w = e * dprob[slot][u, low : low + strip, :]
                e, w = fold(e, jnp.sum), fold(w, jnp.sum)
                total, weighted = (e, w) if total is None else (total + e, weighted + w)
            shrink = jnp.exp2(top_conv - top)
            total = stats[h, 1:2, :] * shrink + jnp.sum(total, axis=0, keepdims=True)
            weighted = stats[h, 2:3, :] * shrink + jnp.sum(weighted, axis=0, keepdims=True)
            inverse = 1.0 / total
            delta = weighted * inverse
            cols = slice(u * tokens, (u + 1) * tokens)
            for low in range(0, cart, strip):
                p = score[slot][u, low : low + strip, :] * inverse
                probs[slot][low : low + strip, cols] = p.astype(jnp.bfloat16)
                ds = p * (dprob[slot][u, low : low + strip, :] - delta)
                dscore[slot][low : low + strip, cols] = ds.astype(jnp.bfloat16)

    def cart_grads(pair, slot):
        g, j = place_of(pair)
        for kind, (left, right) in enumerate(((dscore, q_s), (probs, og_s))):
            both = jnp.concatenate([right[:, head_cols(g, j + u)] for u in range(2)], axis=0)
            term = dot(left[slot][...], both).reshape(half, 2, rows, HD)
            part[g, :, :, kind] += term

    part[...] = jnp.zeros_like(part)
    for ref in (probs_b, dscore_b):
        ref[...] = jnp.zeros_like(ref)
    peers = [lax.rem(me + 2 * i, n) for i in range(half)]
    def pair_copy(g):
        return remote(
            part.at[g, :, 1 - core], r1.at[g], s1_send.at[g], s1_recv.at[g], (dp, sibling)
        )

    def place_copy(g, i):
        return remote(
            s2.at[g, i], r2.at[g, i], s2_send.at[g, i], s2_recv.at[g, i], (dp, peers[i])
        )

    def all_copy(g, i):
        return remote(
            r3.at[g, dp], r3.at[g, dp], s3_send.at[g, i], s3_recv.at[g, i],
            (lax.rem(dp + i, nd), me),
        )

    def start_place(g):
        pair_copy(g).wait_recv()
        for i in range(1, half):
            to = lax.rem(place + i, half)
            s2[g, i] = (part[g, to, core] + r1[g, to]).astype(jnp.bfloat16)
            place_copy(g, i).start()

    def start_all(g):
        total = part[g, place, core] + r1[g, place]
        for i in range(1, half):
            place_copy(g, i).wait_recv()
            total = total + r2[g, i].astype(jnp.float32)
        r3[g, dp] = total.astype(jnp.bfloat16)
        for i in range(1, nd):
            all_copy(g, i).start()

    def finish(g):
        for i in range(1, nd):
            all_copy(g, i).wait_recv()
        total = r3[g, 0].astype(jnp.float32)
        for i in range(1, nd):
            total = total + r3[g, i].astype(jnp.float32)
        out_ref[:, :, g * HD : (g + 1) * HD] = total

    def cart_step(step):
        g, late = step // 2, lax.rem(step, 2) == 1

        @pl.when(late & (g + 1 < groups))
        def _():
            gathered(g + 1)

        for i in range(per):
            cart_grads(step * per + i - 1, (i + 1) % 2)
            cart_products(step * per + i + 1, (i + 1) % 2)
            cart_probs(step * per + i, i % 2)

        @pl.when(jnp.logical_not(late) & (g >= 1))
        def _():
            pair_copy(g - 1).start()

        @pl.when(late & (g >= 1))
        def _():
            start_place(g - 1)

        @pl.when(jnp.logical_not(late) & (g >= 2))
        def _():
            start_all(g - 2)

    gathered(0)
    cart_products(0, 0)
    pl.loop(0, 2 * groups)(cart_step)
    cart_grads(pairs - 1, 1)
    pair_copy(groups - 1).start()
    start_place(groups - 1)
    if groups > 1:
        start_all(groups - 2)
    for g in range(groups - 1):
        finish(g)
    start_all(groups - 1)
    finish(groups - 1)

    for g in range(groups):
        for i in range(1, half):
            gather(g, i).wait_send()
        for i in range(half):
            forward(g, i).wait_send()
        pair_copy(g).wait_send()
        for i in range(1, half):
            place_copy(g, i).wait_send()
        for i in range(1, nd):
            all_copy(g, i).wait_send()


def solution(mesh):
    n, nd = mesh.shape["ctx"], mesh.shape["dp"]

    def per_device(queries, conv_keys, conv_values, out_grad, segment_ids, cart_keys, cart_values):
        tokens = queries.shape[0]
        rows = cart_keys.shape[0]
        groups = cart_keys.shape[1] // HD
        heads = queries.shape[1] // (groups * HD)
        half = n // 2
        bf16, f32 = jnp.bfloat16, jnp.float32
        dma = pltpu.SemaphoreType.DMA
        scratch = [
            pltpu.VMEM(queries.shape, bf16),
            pltpu.VMEM(out_grad.shape, bf16),
            pltpu.VMEM(conv_keys.shape, bf16),
            pltpu.VMEM(conv_values.shape, bf16),
            pltpu.VMEM(segment_ids.shape, jnp.int32),
            pltpu.VMEM((tokens, tokens), f32),
            pltpu.VMEM((groups * heads, 8, tokens), f32),
            pltpu.VMEM((groups, n, 2, rows, HD), bf16),
            pltpu.VMEM((groups, half, 2, 2, rows, HD), f32),
            pltpu.VMEM((groups, half, 2, rows, HD), f32),
            pltpu.VMEM((groups, half, 2, rows, HD), bf16),
            pltpu.VMEM((groups, half, 2, rows, HD), bf16),
            pltpu.VMEM((groups, nd, 2, rows, HD), bf16),
            *[pltpu.VMEM((2, max(n * rows, tokens), tokens), f32)] * 4,
            *[pltpu.VMEM((8, tokens), f32)] * 2,
            *[pltpu.VMEM((n * rows, 2 * tokens), bf16)] * 4,
            dma((2, groups)),
            dma((3,)),
            dma((2, groups)),
            *[dma((groups, half))] * 4,
            dma((groups,)),
            dma((groups,)),
            dma((groups, half)),
            dma((groups, half)),
            dma((groups, nd)),
            dma((groups, nd)),
        ]
        out = pl.pallas_call(
            functools.partial(kernel, n, nd, groups, heads),
            out_shape=jax.ShapeDtypeStruct((2, *cart_keys.shape), f32),
            in_specs=[pl.BlockSpec(memory_space=pltpu.HBM)] * 7,
            out_specs=pl.BlockSpec(memory_space=pltpu.VMEM),
            scratch_shapes=scratch,
            compiler_params=pltpu.CompilerParams(
                collective_id=0, has_side_effects=True, vmem_limit_bytes=64 * 1024 * 1024
            ),
        )(queries, conv_keys, conv_values, out_grad, segment_ids, cart_keys, cart_values)
        return out[0] * (1.0 / math.sqrt(HD)), out[1]

    in_specs = (P(("dp", "ctx"), None),) * 5 + (P("ctx", None),) * 2
    out_specs = (P("ctx", None), P("ctx", None))
    return jax.shard_map(
        per_device, mesh=mesh, in_specs=in_specs, out_specs=out_specs, check_vma=False
    )
```

```python
import functools
import math

import jax
import jax.numpy as jnp
from jax import lax
from jax.experimental import pallas as pl
from jax.experimental.pallas import tpu as pltpu
from jax.sharding import PartitionSpec as P

HD = 128
MESH = pl.DeviceIdType.MESH


def dot(a, b):
    return jnp.dot(a, b, preferred_element_type=jnp.float32)


def kernel(
    n, nd, groups, heads,
    q_hbm, ck_hbm, cv_hbm, og_hbm, seg_hbm, kk_hbm, kv_hbm,
    out_ref,
    q_s, og_s, q_t, og_t, ck_s, cv_s, seg_s, bias, stats, buf, part, r1, s2, r2, r3,
    score_a, score_b, dprob_a, dprob_b, tops_a, tops_b, probs_a, probs_b, dscore_a, dscore_b,
    in_sem, conv_sem, cart_sem,
    g_send, g_recv, f_send, f_recv, s1_send, s1_recv, s2_send, s2_recv, s3_send, s3_recv,
):
    dp, me = lax.axis_index("dp"), lax.axis_index("ctx")
    half = n // 2
    core = lax.rem(me, 2)
    place = me // 2
    sibling = me + 1 - 2 * core
    tokens = q_s.shape[0]
    rows = buf.shape[3]
    cart = n * rows
    width = heads * HD
    factor = math.log2(math.e) / math.sqrt(HD)

    score, dprob, tops = (score_a, score_b), (dprob_a, dprob_b), (tops_a, tops_b)
    probs, dscore = (probs_a, probs_b), (dscore_a, dscore_b)

    barrier = pltpu.get_barrier_semaphore()
    pl.semaphore_signal(barrier, inc=1, device_id=(dp, sibling), device_id_type=MESH)
    for i in range(1, half):
        pl.semaphore_signal(
            barrier, inc=1, device_id=(dp, lax.rem(me + 2 * i, n)), device_id_type=MESH
        )
    for i in range(1, nd):
        pl.semaphore_signal(
            barrier, inc=1, device_id=(lax.rem(dp + i, nd), me), device_id_type=MESH
        )

    cart_copies = []
    for g in range(groups):
        cols = pl.ds(g * HD, HD)
        for kind, ref in enumerate((kk_hbm, kv_hbm)):
            cart_copies.append(
                pltpu.make_async_copy(
                    ref.at[:, cols], buf.at[g, me, kind], cart_sem.at[kind, g]
                )
            )
    for copy in cart_copies:
        copy.start()
    conv_copies = [
        pltpu.make_async_copy(seg_hbm, seg_s, conv_sem.at[0]),
        pltpu.make_async_copy(ck_hbm, ck_s, conv_sem.at[1]),
        pltpu.make_async_copy(cv_hbm, cv_s, conv_sem.at[2]),
    ]
    for copy in conv_copies:
        copy.start()

    def in_copies(g):
        cols = pl.ds(pl.multiple_of(g * width, width), width)
        return [
            pltpu.make_async_copy(q_hbm.at[:, cols], q_s.at[:, cols], in_sem.at[0, g]),
            pltpu.make_async_copy(og_hbm.at[:, cols], og_s.at[:, cols], in_sem.at[1, g]),
        ]

    for g in range(groups):
        for copy in in_copies(g):
            copy.start()
    for copy in cart_copies:
        copy.wait()
    pl.semaphore_wait(barrier, 1 + (half - 1) + (nd - 1))

    def remote(src, dst, send, recv, target):
        return pltpu.make_async_remote_copy(
            src_ref=src, dst_ref=dst, send_sem=send, recv_sem=recv,
            device_id=target, device_id_type=MESH,
        )

    def gather(g, i):
        return remote(
            buf.at[g, me], buf.at[g, me], g_send.at[g, i], g_recv.at[g, i],
            (dp, lax.rem(me + 2 * i, n)),
        )

    def forward(g, i):
        chunk = buf.at[g, lax.rem(me + n - 2 * i, n)]
        return remote(chunk, chunk, f_send.at[g, i], f_recv.at[g, i], (dp, sibling))

    def pass_on(g):
        for i in range(1, half):
            gather(g, i).wait_recv()
            forward(g, i).start()

    def gathered(g):
        for i in range(half):
            forward(g, i).wait_recv()

    for g in range(groups):
        for i in range(1, half):
            gather(g, i).start()
        forward(g, 0).start()

    for copy in conv_copies:
        copy.wait()
    seg_row = jnp.broadcast_to(seg_s[...].astype(jnp.float32), (tokens, tokens))
    key_at = lax.broadcasted_iota(jnp.int32, (tokens, tokens), 0)
    token_at = lax.broadcasted_iota(jnp.int32, (tokens, tokens), 1)
    allowed = (seg_row == seg_row.T) & (key_at <= token_at)
    bias[...] = jnp.where(allowed, 0.0, -1e30)
    mid = tokens // 2

    strip = 32

    def fold(x, reduce):
        return reduce(x.reshape(x.shape[0] // 8, 8, x.shape[1]), axis=0)

    def head_cols(g, j):
        return pl.ds(pl.multiple_of(g * width + j * HD, HD), HD)

    def conv_products(g, j, slot):
        cols, own = head_cols(g, j), pl.ds(pl.multiple_of(g * HD, HD), HD)
        h = g * heads + j
        q, og = q_s[:, cols].T, og_s[:, cols].T
        q_t[h], og_t[h] = q, og
        s0 = dot(ck_s[:mid, own], q) + bias[:mid, :]
        s1 = dot(ck_s[mid:, own], q[:, mid:]) + bias[mid:, mid:]
        score[slot][:mid, :] = s0
        score[slot][mid:tokens, mid:] = s1
        dprob[slot][:mid, :] = dot(cv_s[:mid, own], og)
        dprob[slot][mid:tokens, mid:] = dot(cv_s[mid:, own], og[:, mid:])
        top0 = jnp.max(fold(s0, jnp.max), axis=0, keepdims=True)
        top1 = jnp.max(fold(s1, jnp.max), axis=0, keepdims=True)
        tops[slot][0:1, :] = jnp.concatenate(
            [top0[:, :mid], jnp.maximum(top0[:, mid:], top1)], axis=1
        ) * factor

    def conv_sums(g, j, slot):
        top = tops[slot][0:1, :]
        total = weighted = None
        for low in range(0, mid, strip):
            e = jnp.exp2(score[slot][low : low + strip, :] * factor - top)
            w = e * dprob[slot][low : low + strip, :]
            e, w = fold(e, jnp.sum), fold(w, jnp.sum)
            total, weighted = (e, w) if total is None else (total + e, weighted + w)
        late_total = late_weighted = None
        for low in range(mid, tokens, strip):
            e = jnp.exp2(score[slot][low : low + strip, mid:] * factor - top[:, mid:])
            w = e * dprob[slot][low : low + strip, mid:]
            e, w = fold(e, jnp.sum), fold(w, jnp.sum)
            late_total, late_weighted = (
                (e, w) if late_total is None else (late_total + e, late_weighted + w)
            )

        def whole(early, late):
            both = jnp.concatenate([early[:, :mid], early[:, mid:] + late], axis=1)
            return jnp.sum(both, axis=0, keepdims=True)

        h = g * heads + j
        stats[h, 0:1, :] = top
        stats[h, 1:2, :] = whole(total, late_total)
        stats[h, 2:3, :] = whole(weighted, late_weighted)

    per = heads // 2

    def next_of(step, j):
        head = jnp.minimum(step * per + j + 1, groups * heads - 1)
        return head // heads, lax.rem(head, heads)

    def conv_step(step):
        g, first = step // 2, lax.rem(step, 2) * per

        @pl.when((first > 0) & (g + 1 < groups))
        def _():
            for copy in in_copies(g + 1):
                copy.wait()

        for j in range(per):
            conv_products(*next_of(step, j), (j + 1) % 2)
            conv_sums(g, first + j, j % 2)

        @pl.when((first > 0) & (g >= 1))
        def _():
            pass_on(g - 1)

    for copy in in_copies(0):
        copy.wait()
    conv_products(0, 0, 0)
    pl.loop(0, 2 * groups)(conv_step)
    pass_on(groups - 1)

    def cart_products(g, j, slot):
        h = g * heads + j
        s = dot(buf[g, :, 0].reshape(cart, HD), q_t[h])
        score[slot][:cart, :] = s
        tops[slot][0:1, :] = jnp.max(fold(s, jnp.max), axis=0, keepdims=True) * factor
        dprob[slot][:cart, :] = dot(buf[g, :, 1].reshape(cart, HD), og_t[h])

    def cart_probs(g, j, slot):
        h = g * heads + j
        top_conv = stats[h, 0:1, :]
        top = jnp.maximum(tops[slot][0:1, :], top_conv)
        total = weighted = None
        for low in range(0, cart, strip):
            e = jnp.exp2(score[slot][low : low + strip, :] * factor - top)
            score[slot][low : low + strip, :] = e
            w = e * dprob[slot][low : low + strip, :]
            e, w = fold(e, jnp.sum), fold(w, jnp.sum)
            total, weighted = (e, w) if total is None else (total + e, weighted + w)
        shrink = jnp.exp2(top_conv - top)
        total = stats[h, 1:2, :] * shrink + jnp.sum(total, axis=0, keepdims=True)
        weighted = stats[h, 2:3, :] * shrink + jnp.sum(weighted, axis=0, keepdims=True)
        inverse = 1.0 / total
        delta = weighted * inverse
        for low in range(0, cart, strip):
            p = score[slot][low : low + strip, :] * inverse
            probs[slot][low : low + strip, :] = p.astype(jnp.bfloat16)
            ds = p * (dprob[slot][low : low + strip, :] - delta)
            dscore[slot][low : low + strip, :] = ds.astype(jnp.bfloat16)

    def cart_grads(g, j, slot):
        cols = head_cols(g, j)
        for kind, (left, right) in enumerate(((dscore, q_s), (probs, og_s))):
            term = dot(left[slot][...], right[:, cols]).reshape(half, 2, rows, HD)
            part[g, :, :, kind] += term

    part[...] = jnp.zeros_like(part)
    peers = [lax.rem(me + 2 * i, n) for i in range(half)]
    def pair_copy(g):
        return remote(
            part.at[g, :, 1 - core], r1.at[g], s1_send.at[g], s1_recv.at[g], (dp, sibling)
        )

    def place_copy(g, i):
        return remote(
            s2.at[g, i], r2.at[g, i], s2_send.at[g, i], s2_recv.at[g, i], (dp, peers[i])
        )

    def all_copy(g, i):
        return remote(
            r3.at[g, dp], r3.at[g, dp], s3_send.at[g, i], s3_recv.at[g, i],
            (lax.rem(dp + i, nd), me),
        )

    def start_place(g):
        pair_copy(g).wait_recv()
        for i in range(1, half):
            to = lax.rem(place + i, half)
            s2[g, i] = (part[g, to, core] + r1[g, to]).astype(jnp.bfloat16)
            place_copy(g, i).start()

    def start_all(g):
        total = part[g, place, core] + r1[g, place]
        for i in range(1, half):
            place_copy(g, i).wait_recv()
            total = total + r2[g, i].astype(jnp.float32)
        r3[g, dp] = total.astype(jnp.bfloat16)
        for i in range(1, nd):
            all_copy(g, i).start()

    def finish(g):
        for i in range(1, nd):
            all_copy(g, i).wait_recv()
        total = r3[g, 0].astype(jnp.float32)
        for i in range(1, nd):
            total = total + r3[g, i].astype(jnp.float32)
        out_ref[:, :, g * HD : (g + 1) * HD] = total

    def cart_step(step):
        g, first = step // 2, lax.rem(step, 2) * per

        @pl.when((first > 0) & (g + 1 < groups))
        def _():
            gathered(g + 1)

        for j in range(per):
            cart_products(*next_of(step, j), (j + 1) % 2)
            cart_probs(g, first + j, j % 2)
            cart_grads(g, first + j, j % 2)

        @pl.when(first > 0)
        def _():
            pair_copy(g).start()

        @pl.when((first == 0) & (g >= 1))
        def _():
            start_place(g - 1)

        @pl.when((first == 0) & (g >= 2))
        def _():
            start_all(g - 2)

    gathered(0)
    cart_products(0, 0, 0)
    pl.loop(0, 2 * groups)(cart_step)
    start_place(groups - 1)
    if groups > 1:
        start_all(groups - 2)
    for g in range(groups - 1):
        finish(g)
    start_all(groups - 1)
    finish(groups - 1)

    for g in range(groups):
        for i in range(1, half):
            gather(g, i).wait_send()
        for i in range(half):
            forward(g, i).wait_send()
        pair_copy(g).wait_send()
        for i in range(1, half):
            place_copy(g, i).wait_send()
        for i in range(1, nd):
            all_copy(g, i).wait_send()


def solution(mesh):
    n, nd = mesh.shape["ctx"], mesh.shape["dp"]

    def per_device(queries, conv_keys, conv_values, out_grad, segment_ids, cart_keys, cart_values):
        tokens = queries.shape[0]
        rows = cart_keys.shape[0]
        groups = cart_keys.shape[1] // HD
        heads = queries.shape[1] // (groups * HD)
        half = n // 2
        bf16, f32 = jnp.bfloat16, jnp.float32
        dma = pltpu.SemaphoreType.DMA
        scratch = [
            pltpu.VMEM(queries.shape, bf16),
            pltpu.VMEM(out_grad.shape, bf16),
            *[pltpu.VMEM((groups * heads, HD, tokens), bf16)] * 2,
            pltpu.VMEM(conv_keys.shape, bf16),
            pltpu.VMEM(conv_values.shape, bf16),
            pltpu.VMEM(segment_ids.shape, jnp.int32),
            pltpu.VMEM((tokens, tokens), f32),
            pltpu.VMEM((groups * heads, 8, tokens), f32),
            pltpu.VMEM((groups, n, 2, rows, HD), bf16),
            pltpu.VMEM((groups, half, 2, 2, rows, HD), f32),
            pltpu.VMEM((groups, half, 2, rows, HD), f32),
            pltpu.VMEM((groups, half, 2, rows, HD), bf16),
            pltpu.VMEM((groups, half, 2, rows, HD), bf16),
            pltpu.VMEM((groups, nd, 2, rows, HD), bf16),
            *[pltpu.VMEM((max(n * rows, tokens), tokens), f32)] * 4,
            *[pltpu.VMEM((8, tokens), f32)] * 2,
            *[pltpu.VMEM((n * rows, tokens), bf16)] * 4,
            dma((2, groups)),
            dma((3,)),
            dma((2, groups)),
            *[dma((groups, half))] * 4,
            dma((groups,)),
            dma((groups,)),
            dma((groups, half)),
            dma((groups, half)),
            dma((groups, nd)),
            dma((groups, nd)),
        ]
        out = pl.pallas_call(
            functools.partial(kernel, n, nd, groups, heads),
            out_shape=jax.ShapeDtypeStruct((2, *cart_keys.shape), f32),
            in_specs=[pl.BlockSpec(memory_space=pltpu.HBM)] * 7,
            out_specs=pl.BlockSpec(memory_space=pltpu.VMEM),
            scratch_shapes=scratch,
            compiler_params=pltpu.CompilerParams(
                collective_id=0, has_side_effects=True, vmem_limit_bytes=64 * 1024 * 1024
            ),
        )(queries, conv_keys, conv_values, out_grad, segment_ids, cart_keys, cart_values)
        return out[0] * (1.0 / math.sqrt(HD)), out[1]

    in_specs = (P(("dp", "ctx"), None),) * 5 + (P("ctx", None),) * 2
    out_specs = (P("ctx", None), P("ctx", None))
    return jax.shard_map(
        per_device, mesh=mesh, in_specs=in_specs, out_specs=out_specs, check_vma=False
    )
```

```python
import functools
import math

import jax
import jax.numpy as jnp
from jax import lax
from jax.experimental import pallas as pl
from jax.experimental.pallas import tpu as pltpu
from jax.sharding import PartitionSpec as P

HD = 128
MESH = pl.DeviceIdType.MESH
NT = (((1,), (1,)), ((), ()))


def dot_nt(a, b):
    return lax.dot_general(a, b, NT, preferred_element_type=jnp.float32)


def dot(a, b):
    return jnp.dot(a, b, preferred_element_type=jnp.float32)


def kernel(
    n, nd, groups, heads,
    q_hbm, ck_hbm, cv_hbm, og_hbm, seg_hbm, kk_hbm, kv_hbm,
    out_ref,
    q_s, og_s, ck_s, cv_s, seg_s, bias, buf, part, r1, s2, r2, r3,
    score_a, score_b, dprob_a, dprob_b, tops_a, tops_b, probs_a, probs_b, dscore_a, dscore_b,
    in_sem, conv_sem, cart_sem,
    g_send, g_recv, f_send, f_recv, s1_send, s1_recv, s2_send, s2_recv, s3_send, s3_recv,
):
    dp, me = lax.axis_index("dp"), lax.axis_index("ctx")
    half = n // 2
    core = lax.rem(me, 2)
    place = me // 2
    sibling = me + 1 - 2 * core
    tokens = q_s.shape[0]
    rows = buf.shape[3]
    cart = n * rows
    width = heads * HD
    factor = math.log2(math.e) / math.sqrt(HD)

    score, dprob, tops = (score_a, score_b), (dprob_a, dprob_b), (tops_a, tops_b)
    probs, dscore = (probs_a, probs_b), (dscore_a, dscore_b)

    barrier = pltpu.get_barrier_semaphore()
    pl.semaphore_signal(barrier, inc=1, device_id=(dp, sibling), device_id_type=MESH)
    for i in range(1, half):
        pl.semaphore_signal(
            barrier, inc=1, device_id=(dp, lax.rem(me + 2 * i, n)), device_id_type=MESH
        )
    for i in range(1, nd):
        pl.semaphore_signal(
            barrier, inc=1, device_id=(lax.rem(dp + i, nd), me), device_id_type=MESH
        )

    cart_copies = []
    for g in range(groups):
        cols = pl.ds(g * HD, HD)
        for kind, ref in enumerate((kk_hbm, kv_hbm)):
            cart_copies.append(
                pltpu.make_async_copy(
                    ref.at[:, cols], buf.at[g, me, kind], cart_sem.at[kind, g]
                )
            )
    for copy in cart_copies:
        copy.start()
    conv_copies = [
        pltpu.make_async_copy(seg_hbm, seg_s, conv_sem.at[0]),
        pltpu.make_async_copy(ck_hbm, ck_s, conv_sem.at[1]),
        pltpu.make_async_copy(cv_hbm, cv_s, conv_sem.at[2]),
    ]
    for copy in conv_copies:
        copy.start()

    def in_copies(g):
        cols = pl.ds(pl.multiple_of(g * width, width), width)
        return [
            pltpu.make_async_copy(q_hbm.at[:, cols], q_s.at[:, cols], in_sem.at[0, g]),
            pltpu.make_async_copy(og_hbm.at[:, cols], og_s.at[:, cols], in_sem.at[1, g]),
        ]

    for g in range(groups):
        for copy in in_copies(g):
            copy.start()
    for copy in cart_copies:
        copy.wait()
    pl.semaphore_wait(barrier, 1 + (half - 1) + (nd - 1))

    def remote(src, dst, send, recv, target):
        return pltpu.make_async_remote_copy(
            src_ref=src, dst_ref=dst, send_sem=send, recv_sem=recv,
            device_id=target, device_id_type=MESH,
        )

    def gather(g, i):
        return remote(
            buf.at[g, me], buf.at[g, me], g_send.at[g, i], g_recv.at[g, i],
            (dp, lax.rem(me + 2 * i, n)),
        )

    def forward(g, i):
        chunk = buf.at[g, lax.rem(me + n - 2 * i, n)]
        return remote(chunk, chunk, f_send.at[g, i], f_recv.at[g, i], (dp, sibling))

    def pass_on(g):
        for i in range(1, half):
            gather(g, i).wait_recv()
            forward(g, i).start()

    def gathered(g):
        for i in range(half):
            forward(g, i).wait_recv()

    for g in range(groups):
        for i in range(1, half):
            gather(g, i).start()
        forward(g, 0).start()

    for copy in conv_copies:
        copy.wait()
    seg_row = jnp.broadcast_to(seg_s[...].astype(jnp.float32), (tokens, tokens))
    key_at = lax.broadcasted_iota(jnp.int32, (tokens, tokens), 0)
    token_at = lax.broadcasted_iota(jnp.int32, (tokens, tokens), 1)
    allowed = (seg_row == seg_row.T) & (key_at <= token_at)
    bias[...] = jnp.where(allowed, 0.0, -1e30)
    mid = tokens // 2

    strip = 32

    def fold(x, reduce):
        return reduce(x.reshape(x.shape[0] // 8, 8, x.shape[1]), axis=0)

    def head_cols(g, j):
        return pl.ds(pl.multiple_of(g * width + j * HD, HD), HD)

    def products(g, j, slot):
        cols, own = head_cols(g, j), pl.ds(pl.multiple_of(g * HD, HD), HD)
        keys = jnp.concatenate([buf[g, :, 0].reshape(cart, HD), ck_s[:, own]], axis=0)
        values = jnp.concatenate([buf[g, :, 1].reshape(cart, HD), cv_s[:, own]], axis=0)
        s = dot_nt(keys, q_s[:, cols])
        conv = s[cart:] + bias[...]
        score[slot][:cart, :] = s[:cart]
        score[slot][cart:, :] = conv
        top = jnp.maximum(fold(s[:cart], jnp.max), fold(conv, jnp.max))
        tops[slot][0:1, :] = jnp.max(top, axis=0, keepdims=True) * factor
        dprob[slot][...] = dot_nt(values, og_s[:, cols])

    def softmax(slot):
        top = tops[slot][0:1, :]

        def sums(low, lanes):
            e = jnp.exp2(score[slot][low : low + strip, lanes] * factor - top[:, lanes])
            w = e * dprob[slot][low : low + strip, lanes]
            return e, fold(e, jnp.sum), fold(w, jnp.sum)

        total = weighted = 0.0
        for low in range(0, cart + mid, strip):
            e, e_sum, w_sum = sums(low, slice(0, tokens))
            if low < cart:
                score[slot][low : low + strip, :] = e
            total, weighted = total + e_sum, weighted + w_sum
        late_total = late_weighted = 0.0
        for low in range(cart + mid, cart + tokens, strip):
            _, e_sum, w_sum = sums(low, slice(mid, tokens))
            late_total, late_weighted = late_total + e_sum, late_weighted + w_sum

        def whole(early, late):
            both = jnp.concatenate([early[:, :mid], early[:, mid:] + late], axis=1)
            return jnp.sum(both, axis=0, keepdims=True)

        inverse = 1.0 / whole(total, late_total)
        delta = whole(weighted, late_weighted) * inverse
        for low in range(0, cart, strip):
            p = score[slot][low : low + strip, :] * inverse
            probs[slot][low : low + strip, :] = p.astype(jnp.bfloat16)
            ds = p * (dprob[slot][low : low + strip, :] - delta)
            dscore[slot][low : low + strip, :] = ds.astype(jnp.bfloat16)

    per = heads // 2

    def next_of(step, j):
        head = jnp.minimum(step * per + j + 1, groups * heads - 1)
        return head // heads, lax.rem(head, heads)

    def cart_grads(g, j, slot):
        cols = head_cols(g, j)
        for kind, (left, right) in enumerate(((dscore, q_s), (probs, og_s))):
            term = dot(left[slot][...], right[:, cols]).reshape(half, 2, rows, HD)
            part[g, :, :, kind] += term

    part[...] = jnp.zeros_like(part)
    peers = [lax.rem(me + 2 * i, n) for i in range(half)]
    def pair_copy(g):
        return remote(
            part.at[g, :, 1 - core], r1.at[g], s1_send.at[g], s1_recv.at[g], (dp, sibling)
        )

    def place_copy(g, i):
        return remote(
            s2.at[g, i], r2.at[g, i], s2_send.at[g, i], s2_recv.at[g, i], (dp, peers[i])
        )

    def all_copy(g, i):
        return remote(
            r3.at[g, dp], r3.at[g, dp], s3_send.at[g, i], s3_recv.at[g, i],
            (lax.rem(dp + i, nd), me),
        )

    def start_place(g):
        pair_copy(g).wait_recv()
        for i in range(1, half):
            to = lax.rem(place + i, half)
            s2[g, i] = (part[g, to, core] + r1[g, to]).astype(jnp.bfloat16)
            place_copy(g, i).start()

    def start_all(g):
        total = part[g, place, core] + r1[g, place]
        for i in range(1, half):
            place_copy(g, i).wait_recv()
            total = total + r2[g, i].astype(jnp.float32)
        r3[g, dp] = total.astype(jnp.bfloat16)
        for i in range(1, nd):
            all_copy(g, i).start()

    def finish(g):
        for i in range(1, nd):
            all_copy(g, i).wait_recv()
        total = r3[g, 0].astype(jnp.float32)
        for i in range(1, nd):
            total = total + r3[g, i].astype(jnp.float32)
        out_ref[:, :, g * HD : (g + 1) * HD] = total

    def step_body(step):
        g, first = step // 2, lax.rem(step, 2) * per

        @pl.when((first == 0) & (g + 1 < groups))
        def _():
            pass_on(g + 1)

        @pl.when((first > 0) & (g + 1 < groups))
        def _():
            for copy in in_copies(g + 1):
                copy.wait()
            gathered(g + 1)

        for j in range(per):
            products(*next_of(step, j), (j + 1) % 2)
            softmax(j % 2)
            cart_grads(g, first + j, j % 2)

        @pl.when(first > 0)
        def _():
            pair_copy(g).start()

        @pl.when((first == 0) & (g >= 1))
        def _():
            start_place(g - 1)

        @pl.when((first == 0) & (g >= 2))
        def _():
            start_all(g - 2)

    pass_on(0)
    for copy in in_copies(0):
        copy.wait()
    gathered(0)
    products(0, 0, 0)
    pl.loop(0, 2 * groups)(step_body)
    start_place(groups - 1)
    if groups > 1:
        start_all(groups - 2)
    for g in range(groups - 1):
        finish(g)
    start_all(groups - 1)
    finish(groups - 1)

    for g in range(groups):
        for i in range(1, half):
            gather(g, i).wait_send()
        for i in range(half):
            forward(g, i).wait_send()
        pair_copy(g).wait_send()
        for i in range(1, half):
            place_copy(g, i).wait_send()
        for i in range(1, nd):
            all_copy(g, i).wait_send()


def solution(mesh):
    n, nd = mesh.shape["ctx"], mesh.shape["dp"]

    def per_device(queries, conv_keys, conv_values, out_grad, segment_ids, cart_keys, cart_values):
        tokens = queries.shape[0]
        rows = cart_keys.shape[0]
        groups = cart_keys.shape[1] // HD
        heads = queries.shape[1] // (groups * HD)
        half = n // 2
        bf16, f32 = jnp.bfloat16, jnp.float32
        dma = pltpu.SemaphoreType.DMA
        scratch = [
            pltpu.VMEM(queries.shape, bf16),
            pltpu.VMEM(out_grad.shape, bf16),
            pltpu.VMEM(conv_keys.shape, bf16),
            pltpu.VMEM(conv_values.shape, bf16),
            pltpu.VMEM(segment_ids.shape, jnp.int32),
            pltpu.VMEM((tokens, tokens), f32),
            pltpu.VMEM((groups, n, 2, rows, HD), bf16),
            pltpu.VMEM((groups, half, 2, 2, rows, HD), f32),
            pltpu.VMEM((groups, half, 2, rows, HD), f32),
            pltpu.VMEM((groups, half, 2, rows, HD), bf16),
            pltpu.VMEM((groups, half, 2, rows, HD), bf16),
            pltpu.VMEM((groups, nd, 2, rows, HD), bf16),
            *[pltpu.VMEM((n * rows + tokens, tokens), f32)] * 4,
            *[pltpu.VMEM((8, tokens), f32)] * 2,
            *[pltpu.VMEM((n * rows, tokens), bf16)] * 4,
            dma((2, groups)),
            dma((3,)),
            dma((2, groups)),
            *[dma((groups, half))] * 4,
            dma((groups,)),
            dma((groups,)),
            dma((groups, half)),
            dma((groups, half)),
            dma((groups, nd)),
            dma((groups, nd)),
        ]
        out = pl.pallas_call(
            functools.partial(kernel, n, nd, groups, heads),
            out_shape=jax.ShapeDtypeStruct((2, *cart_keys.shape), f32),
            in_specs=[pl.BlockSpec(memory_space=pltpu.HBM)] * 7,
            out_specs=pl.BlockSpec(memory_space=pltpu.VMEM),
            scratch_shapes=scratch,
            compiler_params=pltpu.CompilerParams(
                collective_id=0, has_side_effects=True, vmem_limit_bytes=64 * 1024 * 1024
            ),
        )(queries, conv_keys, conv_values, out_grad, segment_ids, cart_keys, cart_values)
        return out[0] * (1.0 / math.sqrt(HD)), out[1]

    in_specs = (P(("dp", "ctx"), None),) * 5 + (P("ctx", None),) * 2
    out_specs = (P("ctx", None), P("ctx", None))
    return jax.shard_map(
        per_device, mesh=mesh, in_specs=in_specs, out_specs=out_specs, check_vma=False
    )
```

```python
import functools
import math

import jax
import jax.numpy as jnp
from jax import lax
from jax.experimental import pallas as pl
from jax.experimental.pallas import tpu as pltpu
from jax.sharding import PartitionSpec as P

HD = 128
MESH = pl.DeviceIdType.MESH


def dot(a, b):
    return jnp.dot(a, b, preferred_element_type=jnp.float32)


def kernel(
    n, nd, groups, heads,
    q_hbm, ck_hbm, cv_hbm, og_hbm, seg_hbm, kk_hbm, kv_hbm,
    out_ref,
    q_s, og_s, q_t, og_t, ck_s, cv_s, seg_s, bias, stats, buf, part, r1, s2, r2, r3,
    score_a, score_b, dprob_a, dprob_b, tops_a, tops_b, probs_a, probs_b, dscore_a, dscore_b,
    in_sem, conv_sem, cart_sem,
    g_send, g_recv, f_send, f_recv, s1_send, s1_recv, s2_send, s2_recv, s3_send, s3_recv,
):
    dp, me = lax.axis_index("dp"), lax.axis_index("ctx")
    half = n // 2
    core = lax.rem(me, 2)
    place = me // 2
    sibling = me + 1 - 2 * core
    tokens = q_s.shape[0]
    rows = buf.shape[3]
    cart = n * rows
    width = heads * HD
    factor = math.log2(math.e) / math.sqrt(HD)

    score, dprob, tops = (score_a, score_b), (dprob_a, dprob_b), (tops_a, tops_b)
    probs, dscore = (probs_a, probs_b), (dscore_a, dscore_b)

    barrier = pltpu.get_barrier_semaphore()
    pl.semaphore_signal(barrier, inc=1, device_id=(dp, sibling), device_id_type=MESH)
    for i in range(1, half):
        pl.semaphore_signal(
            barrier, inc=1, device_id=(dp, lax.rem(me + 2 * i, n)), device_id_type=MESH
        )
    for i in range(1, nd):
        pl.semaphore_signal(
            barrier, inc=1, device_id=(lax.rem(dp + i, nd), me), device_id_type=MESH
        )

    cart_copies = []
    for g in range(groups):
        cols = pl.ds(g * HD, HD)
        for kind, ref in enumerate((kk_hbm, kv_hbm)):
            cart_copies.append(
                pltpu.make_async_copy(
                    ref.at[:, cols], buf.at[g, me, kind], cart_sem.at[kind, g]
                )
            )
    for copy in cart_copies:
        copy.start()
    conv_copies = [
        pltpu.make_async_copy(seg_hbm, seg_s, conv_sem.at[0]),
        pltpu.make_async_copy(ck_hbm, ck_s, conv_sem.at[1]),
        pltpu.make_async_copy(cv_hbm, cv_s, conv_sem.at[2]),
    ]
    for copy in conv_copies:
        copy.start()

    def in_copies(g):
        cols = pl.ds(pl.multiple_of(g * width, width), width)
        return [
            pltpu.make_async_copy(q_hbm.at[:, cols], q_s.at[:, cols], in_sem.at[0, g]),
            pltpu.make_async_copy(og_hbm.at[:, cols], og_s.at[:, cols], in_sem.at[1, g]),
        ]

    for g in range(groups):
        for copy in in_copies(g):
            copy.start()
    for copy in cart_copies:
        copy.wait()
    pl.semaphore_wait(barrier, 1 + (half - 1) + (nd - 1))

    def remote(src, dst, send, recv, target):
        return pltpu.make_async_remote_copy(
            src_ref=src, dst_ref=dst, send_sem=send, recv_sem=recv,
            device_id=target, device_id_type=MESH,
        )

    def gather(g, i):
        return remote(
            buf.at[g, me], buf.at[g, me], g_send.at[g, i], g_recv.at[g, i],
            (dp, lax.rem(me + 2 * i, n)),
        )

    def forward(g, i):
        chunk = buf.at[g, lax.rem(me + n - 2 * i, n)]
        return remote(chunk, chunk, f_send.at[g, i], f_recv.at[g, i], (dp, sibling))

    def pass_on(g):
        for i in range(1, half):
            gather(g, i).wait_recv()
            forward(g, i).start()

    def gathered(g):
        for i in range(half):
            forward(g, i).wait_recv()

    for g in range(groups):
        for i in range(1, half):
            gather(g, i).start()
        forward(g, 0).start()

    for copy in conv_copies:
        copy.wait()
    seg_row = jnp.broadcast_to(seg_s[...].astype(jnp.float32), (tokens, tokens))
    key_at = lax.broadcasted_iota(jnp.int32, (tokens, tokens), 0)
    token_at = lax.broadcasted_iota(jnp.int32, (tokens, tokens), 1)
    allowed = (seg_row == seg_row.T) & (key_at <= token_at)
    bias[...] = jnp.where(allowed, 0.0, -1e30)
    mid = tokens // 2

    strip = 32

    def fold(x, reduce):
        return reduce(x.reshape(x.shape[0] // 8, 8, x.shape[1]), axis=0)

    def head_cols(g, j):
        return pl.ds(pl.multiple_of(g * width + j * HD, HD), HD)

    def conv_products(g, j, slot):
        cols, own = head_cols(g, j), pl.ds(pl.multiple_of(g * HD, HD), HD)
        h = g * heads + j
        q, og = q_s[:, cols].T, og_s[:, cols].T
        q_t[h], og_t[h] = q, og
        s0 = dot(ck_s[:mid, own], q) + bias[:mid, :]
        s1 = dot(ck_s[mid:, own], q[:, mid:]) + bias[mid:, mid:]
        score[slot][:mid, :] = s0
        score[slot][mid:tokens, mid:] = s1
        dprob[slot][:mid, :] = dot(cv_s[:mid, own], og)
        dprob[slot][mid:tokens, mid:] = dot(cv_s[mid:, own], og[:, mid:])
        top0 = jnp.max(fold(s0, jnp.max), axis=0, keepdims=True)
        top1 = jnp.max(fold(s1, jnp.max), axis=0, keepdims=True)
        tops[slot][0:1, :] = jnp.concatenate(
            [top0[:, :mid], jnp.maximum(top0[:, mid:], top1)], axis=1
        ) * factor

    def conv_sums(g, j, slot):
        top = tops[slot][0:1, :]
        total = weighted = None
        for low in range(0, mid, strip):
            e = jnp.exp2(score[slot][low : low + strip, :] * factor - top)
            w = e * dprob[slot][low : low + strip, :]
            e, w = fold(e, jnp.sum), fold(w, jnp.sum)
            total, weighted = (e, w) if total is None else (total + e, weighted + w)
        late_total = late_weighted = None
        for low in range(mid, tokens, strip):
            e = jnp.exp2(score[slot][low : low + strip, mid:] * factor - top[:, mid:])
            w = e * dprob[slot][low : low + strip, mid:]
            e, w = fold(e, jnp.sum), fold(w, jnp.sum)
            late_total, late_weighted = (
                (e, w) if late_total is None else (late_total + e, late_weighted + w)
            )

        def whole(early, late):
            both = jnp.concatenate([early[:, :mid], early[:, mid:] + late], axis=1)
            return jnp.sum(both, axis=0, keepdims=True)

        h = g * heads + j
        stats[h, 0:1, :] = top
        stats[h, 1:2, :] = whole(total, late_total)
        stats[h, 2:3, :] = whole(weighted, late_weighted)

    per = heads // 2

    def next_of(step, j):
        head = jnp.minimum(step * per + j + 1, groups * heads - 1)
        return head // heads, lax.rem(head, heads)

    def conv_group(g):
        @pl.when(g + 1 < groups)
        def _():
            for copy in in_copies(g + 1):
                copy.wait()

        for j in range(heads):
            conv_products(*next_of(2 * g, j), (j + 1) % 2)
            conv_sums(g, j, j % 2)

        @pl.when(g >= 1)
        def _():
            pass_on(g - 1)

    for copy in in_copies(0):
        copy.wait()
    conv_products(0, 0, 0)
    pl.loop(0, groups)(conv_group)
    pass_on(groups - 1)

    def cart_products(g, j, slot):
        h = g * heads + j
        s = dot(buf[g, :, 0].reshape(cart, HD), q_t[h])
        score[slot][:cart, :] = s
        tops[slot][0:1, :] = jnp.max(fold(s, jnp.max), axis=0, keepdims=True) * factor
        dprob[slot][:cart, :] = dot(buf[g, :, 1].reshape(cart, HD), og_t[h])

    def cart_probs(g, j, slot):
        h = g * heads + j
        top_conv = stats[h, 0:1, :]
        top = jnp.maximum(tops[slot][0:1, :], top_conv)
        total = weighted = None
        for low in range(0, cart, strip):
            e = jnp.exp2(score[slot][low : low + strip, :] * factor - top)
            score[slot][low : low + strip, :] = e
            w = e * dprob[slot][low : low + strip, :]
            e, w = fold(e, jnp.sum), fold(w, jnp.sum)
            total, weighted = (e, w) if total is None else (total + e, weighted + w)
        shrink = jnp.exp2(top_conv - top)
        total = stats[h, 1:2, :] * shrink + jnp.sum(total, axis=0, keepdims=True)
        weighted = stats[h, 2:3, :] * shrink + jnp.sum(weighted, axis=0, keepdims=True)
        inverse = 1.0 / total
        delta = weighted * inverse
        for low in range(0, cart, strip):
            p = score[slot][low : low + strip, :] * inverse
            probs[slot][low : low + strip, :] = p.astype(jnp.bfloat16)
            ds = p * (dprob[slot][low : low + strip, :] - delta)
            dscore[slot][low : low + strip, :] = ds.astype(jnp.bfloat16)

    def cart_grads(g, j, slot):
        cols = head_cols(g, j)
        for kind, (left, right) in enumerate(((dscore, q_s), (probs, og_s))):
            term = dot(left[slot][...], right[:, cols]).reshape(half, 2, rows, HD)
            part[g, :, :, kind] += term

    part[...] = jnp.zeros_like(part)
    peers = [lax.rem(me + 2 * i, n) for i in range(half)]
    def pair_copy(g):
        return remote(
            part.at[g, :, 1 - core], r1.at[g], s1_send.at[g], s1_recv.at[g], (dp, sibling)
        )

    def place_copy(g, i):
        return remote(
            s2.at[g, i], r2.at[g, i], s2_send.at[g, i], s2_recv.at[g, i], (dp, peers[i])
        )

    def all_copy(g, i):
        return remote(
            r3.at[g, dp], r3.at[g, dp], s3_send.at[g, i], s3_recv.at[g, i],
            (lax.rem(dp + i, nd), me),
        )

    def start_place(g):
        pair_copy(g).wait_recv()
        for i in range(1, half):
            to = lax.rem(place + i, half)
            s2[g, i] = (part[g, to, core] + r1[g, to]).astype(jnp.bfloat16)
            place_copy(g, i).start()

    def start_all(g):
        total = part[g, place, core] + r1[g, place]
        for i in range(1, half):
            place_copy(g, i).wait_recv()
            total = total + r2[g, i].astype(jnp.float32)
        r3[g, dp] = total.astype(jnp.bfloat16)
        for i in range(1, nd):
            all_copy(g, i).start()

    def finish(g):
        for i in range(1, nd):
            all_copy(g, i).wait_recv()
        total = r3[g, 0].astype(jnp.float32)
        for i in range(1, nd):
            total = total + r3[g, i].astype(jnp.float32)
        out_ref[:, :, g * HD : (g + 1) * HD] = total

    def cart_step(step):
        g, first = step // 2, lax.rem(step, 2) * per

        @pl.when((first > 0) & (g + 1 < groups))
        def _():
            gathered(g + 1)

        for j in range(per):
            cart_products(*next_of(step, j), (j + 1) % 2)
            if j > 0:
                cart_grads(g, first + j - 1, (j - 1) % 2)
            cart_probs(g, first + j, j % 2)
        cart_grads(g, first + per - 1, (per - 1) % 2)

        @pl.when(first > 0)
        def _():
            pair_copy(g).start()

        @pl.when((first == 0) & (g >= 1))
        def _():
            start_place(g - 1)

        @pl.when((first == 0) & (g >= 2))
        def _():
            start_all(g - 2)

    gathered(0)
    cart_products(0, 0, 0)
    pl.loop(0, 2 * groups)(cart_step)
    start_place(groups - 1)
    if groups > 1:
        start_all(groups - 2)
    for g in range(groups - 1):
        finish(g)
    start_all(groups - 1)
    finish(groups - 1)

    for g in range(groups):
        for i in range(1, half):
            gather(g, i).wait_send()
        for i in range(half):
            forward(g, i).wait_send()
        pair_copy(g).wait_send()
        for i in range(1, half):
            place_copy(g, i).wait_send()
        for i in range(1, nd):
            all_copy(g, i).wait_send()


def solution(mesh):
    n, nd = mesh.shape["ctx"], mesh.shape["dp"]

    def per_device(queries, conv_keys, conv_values, out_grad, segment_ids, cart_keys, cart_values):
        tokens = queries.shape[0]
        rows = cart_keys.shape[0]
        groups = cart_keys.shape[1] // HD
        heads = queries.shape[1] // (groups * HD)
        half = n // 2
        bf16, f32 = jnp.bfloat16, jnp.float32
        dma = pltpu.SemaphoreType.DMA
        scratch = [
            pltpu.VMEM(queries.shape, bf16),
            pltpu.VMEM(out_grad.shape, bf16),
            *[pltpu.VMEM((groups * heads, HD, tokens), bf16)] * 2,
            pltpu.VMEM(conv_keys.shape, bf16),
            pltpu.VMEM(conv_values.shape, bf16),
            pltpu.VMEM(segment_ids.shape, jnp.int32),
            pltpu.VMEM((tokens, tokens), f32),
            pltpu.VMEM((groups * heads, 8, tokens), f32),
            pltpu.VMEM((groups, n, 2, rows, HD), bf16),
            pltpu.VMEM((groups, half, 2, 2, rows, HD), f32),
            pltpu.VMEM((groups, half, 2, rows, HD), f32),
            pltpu.VMEM((groups, half, 2, rows, HD), bf16),
            pltpu.VMEM((groups, half, 2, rows, HD), bf16),
            pltpu.VMEM((groups, nd, 2, rows, HD), bf16),
            *[pltpu.VMEM((max(n * rows, tokens), tokens), f32)] * 4,
            *[pltpu.VMEM((8, tokens), f32)] * 2,
            *[pltpu.VMEM((n * rows, tokens), bf16)] * 4,
            dma((2, groups)),
            dma((3,)),
            dma((2, groups)),
            *[dma((groups, half))] * 4,
            dma((groups,)),
            dma((groups,)),
            dma((groups, half)),
            dma((groups, half)),
            dma((groups, nd)),
            dma((groups, nd)),
        ]
        out = pl.pallas_call(
            functools.partial(kernel, n, nd, groups, heads),
            out_shape=jax.ShapeDtypeStruct((2, *cart_keys.shape), f32),
            in_specs=[pl.BlockSpec(memory_space=pltpu.HBM)] * 7,
            out_specs=pl.BlockSpec(memory_space=pltpu.VMEM),
            scratch_shapes=scratch,
            compiler_params=pltpu.CompilerParams(
                collective_id=0, has_side_effects=True, vmem_limit_bytes=64 * 1024 * 1024
            ),
        )(queries, conv_keys, conv_values, out_grad, segment_ids, cart_keys, cart_values)
        return out[0] * (1.0 / math.sqrt(HD)), out[1]

    in_specs = (P(("dp", "ctx"), None),) * 5 + (P("ctx", None),) * 2
    out_specs = (P("ctx", None), P("ctx", None))
    return jax.shard_map(
        per_device, mesh=mesh, in_specs=in_specs, out_specs=out_specs, check_vma=False
    )
```

```python
import functools
import math

import jax
import jax.numpy as jnp
from jax import lax
from jax.experimental import pallas as pl
from jax.experimental.pallas import tpu as pltpu
from jax.sharding import PartitionSpec as P

HD = 128
MESH = pl.DeviceIdType.MESH


def dot(a, b):
    return jnp.dot(a, b, preferred_element_type=jnp.float32)


def kernel(
    n, nd, groups, heads,
    q_hbm, ck_hbm, cv_hbm, og_hbm, seg_hbm, kk_hbm, kv_hbm,
    out_ref,
    q_s, og_s, q_t, og_t, ck_s, cv_s, seg_s, bias, stats, buf, part, r1, s2, r2, r3,
    score_a, score_b, dprob_a, dprob_b, tops_a, tops_b, probs_a, probs_b, dscore_a, dscore_b,
    in_sem, conv_sem, cart_sem,
    g_send, g_recv, f_send, f_recv, s1_send, s1_recv, s2_send, s2_recv, s3_send, s3_recv,
):
    dp, me = lax.axis_index("dp"), lax.axis_index("ctx")
    half = n // 2
    core = lax.rem(me, 2)
    place = me // 2
    sibling = me + 1 - 2 * core
    tokens = q_s.shape[0]
    rows = buf.shape[3]
    cart = n * rows
    width = heads * HD
    factor = math.log2(math.e) / math.sqrt(HD)

    score, dprob, tops = (score_a, score_b), (dprob_a, dprob_b), (tops_a, tops_b)
    probs, dscore = (probs_a, probs_b), (dscore_a, dscore_b)

    barrier = pltpu.get_barrier_semaphore()
    pl.semaphore_signal(barrier, inc=1, device_id=(dp, sibling), device_id_type=MESH)
    for i in range(1, half):
        pl.semaphore_signal(
            barrier, inc=1, device_id=(dp, lax.rem(me + 2 * i, n)), device_id_type=MESH
        )
    for i in range(1, nd):
        pl.semaphore_signal(
            barrier, inc=1, device_id=(lax.rem(dp + i, nd), me), device_id_type=MESH
        )

    cart_copies = []
    for g in range(groups):
        cols = pl.ds(g * HD, HD)
        for kind, ref in enumerate((kk_hbm, kv_hbm)):
            cart_copies.append(
                pltpu.make_async_copy(
                    ref.at[:, cols], buf.at[g, me, kind], cart_sem.at[kind, g]
                )
            )
    for copy in cart_copies:
        copy.start()
    conv_copies = [
        pltpu.make_async_copy(seg_hbm, seg_s, conv_sem.at[0]),
        pltpu.make_async_copy(ck_hbm, ck_s, conv_sem.at[1]),
        pltpu.make_async_copy(cv_hbm, cv_s, conv_sem.at[2]),
    ]
    for copy in conv_copies:
        copy.start()

    def in_copies(g):
        cols = pl.ds(pl.multiple_of(g * width, width), width)
        return [
            pltpu.make_async_copy(q_hbm.at[:, cols], q_s.at[:, cols], in_sem.at[0, g]),
            pltpu.make_async_copy(og_hbm.at[:, cols], og_s.at[:, cols], in_sem.at[1, g]),
        ]

    for g in range(groups):
        for copy in in_copies(g):
            copy.start()
    for copy in cart_copies:
        copy.wait()
    pl.semaphore_wait(barrier, 1 + (half - 1) + (nd - 1))

    def remote(src, dst, send, recv, target):
        return pltpu.make_async_remote_copy(
            src_ref=src, dst_ref=dst, send_sem=send, recv_sem=recv,
            device_id=target, device_id_type=MESH,
        )

    def gather(g, i):
        return remote(
            buf.at[g, me], buf.at[g, me], g_send.at[g, i], g_recv.at[g, i],
            (dp, lax.rem(me + 2 * i, n)),
        )

    def forward(g, i):
        chunk = buf.at[g, lax.rem(me + n - 2 * i, n)]
        return remote(chunk, chunk, f_send.at[g, i], f_recv.at[g, i], (dp, sibling))

    def pass_on(g):
        for i in range(1, half):
            gather(g, i).wait_recv()
            forward(g, i).start()

    def gathered(g):
        for i in range(half):
            forward(g, i).wait_recv()

    for g in range(groups):
        for i in range(1, half):
            gather(g, i).start()
        forward(g, 0).start()

    for copy in conv_copies:
        copy.wait()
    seg_row = jnp.broadcast_to(seg_s[...].astype(jnp.float32), (tokens, tokens))
    key_at = lax.broadcasted_iota(jnp.int32, (tokens, tokens), 0)
    token_at = lax.broadcasted_iota(jnp.int32, (tokens, tokens), 1)
    allowed = (seg_row == seg_row.T) & (key_at <= token_at)
    bias[...] = jnp.where(allowed, 0.0, -1e30)
    mid = tokens // 2

    strip = 16

    def fold(x, reduce):
        return reduce(x.reshape(x.shape[0] // 8, 8, x.shape[1]), axis=0)

    def head_cols(g, j):
        return pl.ds(pl.multiple_of(g * width + j * HD, HD), HD)

    def conv_products(g, j, slot):
        cols, own = head_cols(g, j), pl.ds(pl.multiple_of(g * HD, HD), HD)
        h = g * heads + j
        q, og = q_s[:, cols].T, og_s[:, cols].T
        q_t[h], og_t[h] = q, og
        s0 = dot(ck_s[:mid, own], q) + bias[:mid, :]
        s1 = dot(ck_s[mid:, own], q[:, mid:]) + bias[mid:, mid:]
        score[slot][:mid, :] = s0
        score[slot][mid:tokens, mid:] = s1
        dprob[slot][:mid, :] = dot(cv_s[:mid, own], og)
        dprob[slot][mid:tokens, mid:] = dot(cv_s[mid:, own], og[:, mid:])
        top0 = jnp.max(fold(s0, jnp.max), axis=0, keepdims=True)
        top1 = jnp.max(fold(s1, jnp.max), axis=0, keepdims=True)
        tops[slot][0:1, :] = jnp.concatenate(
            [top0[:, :mid], jnp.maximum(top0[:, mid:], top1)], axis=1
        ) * factor

    def conv_sums(g, j, slot):
        top = tops[slot][0:1, :]
        total = weighted = None
        for low in range(0, mid, strip):
            e = jnp.exp2(score[slot][low : low + strip, :] * factor - top)
            w = e * dprob[slot][low : low + strip, :]
            e, w = fold(e, jnp.sum), fold(w, jnp.sum)
            total, weighted = (e, w) if total is None else (total + e, weighted + w)
        late_total = late_weighted = None
        for low in range(mid, tokens, strip):
            e = jnp.exp2(score[slot][low : low + strip, mid:] * factor - top[:, mid:])
            w = e * dprob[slot][low : low + strip, mid:]
            e, w = fold(e, jnp.sum), fold(w, jnp.sum)
            late_total, late_weighted = (
                (e, w) if late_total is None else (late_total + e, late_weighted + w)
            )

        def whole(early, late):
            both = jnp.concatenate([early[:, :mid], early[:, mid:] + late], axis=1)
            return jnp.sum(both, axis=0, keepdims=True)

        h = g * heads + j
        stats[h, 0:1, :] = top
        stats[h, 1:2, :] = whole(total, late_total)
        stats[h, 2:3, :] = whole(weighted, late_weighted)

    per = heads // 2

    def next_of(step, j):
        head = jnp.minimum(step * per + j + 1, groups * heads - 1)
        return head // heads, lax.rem(head, heads)

    def conv_step(step):
        g, first = step // 2, lax.rem(step, 2) * per

        @pl.when((first > 0) & (g + 1 < groups))
        def _():
            for copy in in_copies(g + 1):
                copy.wait()

        for j in range(per):
            conv_products(*next_of(step, j), (j + 1) % 2)
            conv_sums(g, first + j, j % 2)

        @pl.when((first > 0) & (g >= 1))
        def _():
            pass_on(g - 1)

    for copy in in_copies(0):
        copy.wait()
    conv_products(0, 0, 0)
    pl.loop(0, 2 * groups)(conv_step)
    pass_on(groups - 1)

    def cart_products(g, j, slot):
        h = g * heads + j
        s = dot(buf[g, :, 0].reshape(cart, HD), q_t[h])
        score[slot][:cart, :] = s
        tops[slot][0:1, :] = jnp.max(fold(s, jnp.max), axis=0, keepdims=True) * factor
        dprob[slot][:cart, :] = dot(buf[g, :, 1].reshape(cart, HD), og_t[h])

    def cart_probs(g, j, slot):
        h = g * heads + j
        top_conv = stats[h, 0:1, :]
        top = jnp.maximum(tops[slot][0:1, :], top_conv)
        total = weighted = None
        for low in range(0, cart, strip):
            e = jnp.exp2(score[slot][low : low + strip, :] * factor - top)
            score[slot][low : low + strip, :] = e
            w = e * dprob[slot][low : low + strip, :]
            e, w = fold(e, jnp.sum), fold(w, jnp.sum)
            total, weighted = (e, w) if total is None else (total + e, weighted + w)
        shrink = jnp.exp2(top_conv - top)
        total = stats[h, 1:2, :] * shrink + jnp.sum(total, axis=0, keepdims=True)
        weighted = stats[h, 2:3, :] * shrink + jnp.sum(weighted, axis=0, keepdims=True)
        inverse = 1.0 / total
        delta = weighted * inverse
        for low in range(0, cart, strip):
            p = score[slot][low : low + strip, :] * inverse
            probs[slot][low : low + strip, :] = p.astype(jnp.bfloat16)
            ds = p * (dprob[slot][low : low + strip, :] - delta)
            dscore[slot][low : low + strip, :] = ds.astype(jnp.bfloat16)

    def cart_grads(g, j, slot):
        cols = head_cols(g, j)
        for kind, (left, right) in enumerate(((dscore, q_s), (probs, og_s))):
            term = dot(left[slot][...], right[:, cols]).reshape(half, 2, rows, HD)
            part[g, :, :, kind] += term

    part[...] = jnp.zeros_like(part)
    peers = [lax.rem(me + 2 * i, n) for i in range(half)]
    def pair_copy(g):
        return remote(
            part.at[g, :, 1 - core], r1.at[g], s1_send.at[g], s1_recv.at[g], (dp, sibling)
        )

    def place_copy(g, i):
        return remote(
            s2.at[g, i], r2.at[g, i], s2_send.at[g, i], s2_recv.at[g, i], (dp, peers[i])
        )

    def all_copy(g, i):
        return remote(
            r3.at[g, dp], r3.at[g, dp], s3_send.at[g, i], s3_recv.at[g, i],
            (lax.rem(dp + i, nd), me),
        )

    def start_place(g):
        pair_copy(g).wait_recv()
        for i in range(1, half):
            to = lax.rem(place + i, half)
            s2[g, i] = (part[g, to, core] + r1[g, to]).astype(jnp.bfloat16)
            place_copy(g, i).start()

    def start_all(g):
        total = part[g, place, core] + r1[g, place]
        for i in range(1, half):
            place_copy(g, i).wait_recv()
            total = total + r2[g, i].astype(jnp.float32)
        r3[g, dp] = total.astype(jnp.bfloat16)
        for i in range(1, nd):
            all_copy(g, i).start()

    def finish(g):
        for i in range(1, nd):
            all_copy(g, i).wait_recv()
        total = r3[g, 0].astype(jnp.float32)
        for i in range(1, nd):
            total = total + r3[g, i].astype(jnp.float32)
        out_ref[:, :, g * HD : (g + 1) * HD] = total

    def cart_step(step):
        g, first = step // 2, lax.rem(step, 2) * per

        @pl.when((first > 0) & (g + 1 < groups))
        def _():
            gathered(g + 1)

        for j in range(per):
            cart_products(*next_of(step, j), (j + 1) % 2)
            cart_probs(g, first + j, j % 2)
            cart_grads(g, first + j, j % 2)

        @pl.when(first > 0)
        def _():
            pair_copy(g).start()

        @pl.when((first == 0) & (g >= 1))
        def _():
            start_place(g - 1)

        @pl.when((first == 0) & (g >= 2))
        def _():
            start_all(g - 2)

    gathered(0)
    cart_products(0, 0, 0)
    pl.loop(0, 2 * groups)(cart_step)
    start_place(groups - 1)
    if groups > 1:
        start_all(groups - 2)
    for g in range(groups - 1):
        finish(g)
    start_all(groups - 1)
    finish(groups - 1)

    for g in range(groups):
        for i in range(1, half):
            gather(g, i).wait_send()
        for i in range(half):
            forward(g, i).wait_send()
        pair_copy(g).wait_send()
        for i in range(1, half):
            place_copy(g, i).wait_send()
        for i in range(1, nd):
            all_copy(g, i).wait_send()


def solution(mesh):
    n, nd = mesh.shape["ctx"], mesh.shape["dp"]

    def per_device(queries, conv_keys, conv_values, out_grad, segment_ids, cart_keys, cart_values):
        tokens = queries.shape[0]
        rows = cart_keys.shape[0]
        groups = cart_keys.shape[1] // HD
        heads = queries.shape[1] // (groups * HD)
        half = n // 2
        bf16, f32 = jnp.bfloat16, jnp.float32
        dma = pltpu.SemaphoreType.DMA
        scratch = [
            pltpu.VMEM(queries.shape, bf16),
            pltpu.VMEM(out_grad.shape, bf16),
            *[pltpu.VMEM((groups * heads, HD, tokens), bf16)] * 2,
            pltpu.VMEM(conv_keys.shape, bf16),
            pltpu.VMEM(conv_values.shape, bf16),
            pltpu.VMEM(segment_ids.shape, jnp.int32),
            pltpu.VMEM((tokens, tokens), f32),
            pltpu.VMEM((groups * heads, 8, tokens), f32),
            pltpu.VMEM((groups, n, 2, rows, HD), bf16),
            pltpu.VMEM((groups, half, 2, 2, rows, HD), f32),
            pltpu.VMEM((groups, half, 2, rows, HD), f32),
            pltpu.VMEM((groups, half, 2, rows, HD), bf16),
            pltpu.VMEM((groups, half, 2, rows, HD), bf16),
            pltpu.VMEM((groups, nd, 2, rows, HD), bf16),
            *[pltpu.VMEM((max(n * rows, tokens), tokens), f32)] * 4,
            *[pltpu.VMEM((8, tokens), f32)] * 2,
            *[pltpu.VMEM((n * rows, tokens), bf16)] * 4,
            dma((2, groups)),
            dma((3,)),
            dma((2, groups)),
            *[dma((groups, half))] * 4,
            dma((groups,)),
            dma((groups,)),
            dma((groups, half)),
            dma((groups, half)),
            dma((groups, nd)),
            dma((groups, nd)),
        ]
        out = pl.pallas_call(
            functools.partial(kernel, n, nd, groups, heads),
            out_shape=jax.ShapeDtypeStruct((2, *cart_keys.shape), f32),
            in_specs=[pl.BlockSpec(memory_space=pltpu.HBM)] * 7,
            out_specs=pl.BlockSpec(memory_space=pltpu.VMEM),
            scratch_shapes=scratch,
            compiler_params=pltpu.CompilerParams(
                collective_id=0, has_side_effects=True, vmem_limit_bytes=64 * 1024 * 1024
            ),
        )(queries, conv_keys, conv_values, out_grad, segment_ids, cart_keys, cart_values)
        return out[0] * (1.0 / math.sqrt(HD)), out[1]

    in_specs = (P(("dp", "ctx"), None),) * 5 + (P("ctx", None),) * 2
    out_specs = (P("ctx", None), P("ctx", None))
    return jax.shard_map(
        per_device, mesh=mesh, in_specs=in_specs, out_specs=out_specs, check_vma=False
    )
```
